32 devices in a mesh: groups: 2 (over y), expert: 4 (over z), replica: 4 (over x, core).
Axes of the slice: x: 2, y: 2, z: 4, core: 2. Of those that a mesh axis runs over, the one named last changes fastest.
Arguments:
- tokens: bfloat16 [4096, 1024], P(('groups', 'expert', 'replica')), parts along dimension 0, may hold values from -6 to 6
- expert_ids: int32 [4096, 6], P(('groups', 'expert', 'replica')), parts along dimension 0, may hold values from 0 to 15, all different within a row; in each aligned block of 128 rows (0 to 127, 128 to 255, ...) at most 64 rows name the same one
- gate_probs: bfloat16 [4096, 6], P(('groups', 'expert', 'replica')), parts along dimension 0, may hold values from 0.099609375 to 0.59765625
- cotangent: bfloat16 [4096, 1024], P(('groups', 'expert', 'replica')), parts along dimension 0, may hold values from -1.5 to 1.5
- gate_up: bfloat16 [1024, 16, 1536], P(None, 'expert'), may hold values from -0.1875 to 0.1875
- down_weights: bfloat16 [768, 16, 1024], P(None, 'expert'), may hold values from -0.21875 to 0.21875
Outputs:
- combined: bfloat16 [4096, 1024], P(('groups', 'expert', 'replica')), parts along dimension 0
- token_gradient: bfloat16 [4096, 1024], P(('groups', 'expert', 'replica')), parts along dimension 0
- prob_gradient: float32 [4096, 6], P(('groups', 'expert', 'replica')), parts along dimension 0
- gate_up_gradient: float32 [2048, 16, 1536], P(('groups', 'replica'), 'expert'), parts along dimension 0
- down_gradient: float32 [1536, 16, 1024], P(('groups', 'replica'), 'expert'), parts along dimension 0
The draws below stay inside these ranges and needn't reach their ends.
There are 2 independent parts, one for each index of `groups`. The reference program is written for one: setup_inputs(seed, part) draws one part's arguments, and reference() takes and returns one part's arrays. A program takes and returns all parts, laid end to end along the dimension named above; an argument that names none is the same for every part. Nothing has to cross between parts.
Inputs may be any that keep to these rules, and one draw needn't show every extreme that they name: `expert_ids`: each row names 6 different experts. Within the rows of one device (aligned blocks of 128 rows) no expert is named by more than 64 rows, and in some block one expert is named by exactly 64 rows.
All inputs are finite; a program needn't handle non-finite values.
Results may differ from the reference program's by a relative error of at most 0.0064.
Values may be sent and summed in bfloat16 or wider, within the bound.
No kernel may reach another device: no remote copies, remote signals or barrier semaphores. Data moves between devices by JAX's collectives and lax.ppermute only.
A program may use at most 128 MiB of HBM per device.

```python
import math
import jax
import jax.numpy as jnp
import numpy as np
from jax import lax

D = 1024
FF = 768
TOP = 6
EXPERTS = 16
TOK_DEV = 128
CAP = 64
TOKENS = 2048
N_EXPERT = 4
N_REPLICA = 4


def level_of(key, shape, split, low, top_value):
    loudness = 1.0
    for dim, shards_of in split:
        draws = jax.random.uniform(jax.random.fold_in(jax.random.fold_in(key, 6), dim), (shards_of,), jnp.float32, low / len(split), top_value / len(split))
        loudness = loudness * jnp.repeat(jnp.exp(draws), shape[dim] // shards_of).reshape((-1,) + (1,) * (len(shape) - 1 - dim))
    return loudness


def assign_block(stream_key, own, number, rows, count, top, reach, slope):
    order = jax.random.permutation(stream_key, count)
    heavy_load, common = portions_of(count, rows * top, reach, slope, True), portions_of(count, rows * top, reach, slope, False)
    places = jnp.arange(count)

    def named(tallies, offset_by):
        used = int((tallies > 0).sum())
        fixed = max(1, used // 4)
        passed = fixed + (places - fixed + offset_by * (used - fixed)) % max(1, count - fixed)
        return jnp.zeros((count,), jnp.int32).at[order[jnp.where(places < fixed, places, passed)]].set(jnp.asarray(tallies, jnp.int32))

    tallies = jnp.where(number % 4 == 0, named(heavy_load, number // 4), named(common, number - number // 4 - 1))
    mixed = jax.random.permutation(jax.random.fold_in(own, 3), count)
    source_of, sink = mixed[0:count // 2 * 2:2], mixed[1:count // 2 * 2:2]
    margin = jnp.minimum(tallies[source_of] - 1, reach - tallies[sink]) // 2
    margin = jnp.where((source_of == order[0]) | (sink == order[0]) | (tallies[sink] == 0), 0, jnp.maximum(margin, 0))
    passed = jax.random.randint(jax.random.fold_in(own, 4), (count // 2,), 0, 1 << 20) % (margin + 1)
    tallies = tallies.at[source_of].add(-passed).at[sink].add(passed)
    members = jnp.searchsorted(jnp.cumsum(tallies), jnp.arange(rows * top), side="right").astype(jnp.int32)
    grid = members.reshape(top, rows).T
    grid = grid[jax.random.permutation(jax.random.fold_in(own, 1), rows)]
    offset_by = jax.random.randint(jax.random.fold_in(own, 2), (rows, 1), 0, top)
    return jnp.take_along_axis(grid, (jnp.arange(top)[None, :] + offset_by) % top, axis=1)


def portions_of(number_of, total, limit, slope, full):
    loads = [(1 << 20) // math.isqrt(grade ** slope) + 1 for grade in range(1, number_of + 1)]
    largest = limit if full else min(limit, max(-(-total // number_of), total * loads[0] // sum(loads)))
    least = 1 if total - largest >= number_of - 1 else 0
    given, rest = [largest] + [least] * (number_of - 1), total - largest - least * (number_of - 1)
    while rest > 0:
        candidates = [i for i in range(1, number_of) if given[i] < largest] or [i for i in range(1, number_of) if given[i] < limit]
        pool, budget = sum([loads[i] for i in candidates]), rest
        for i in candidates:
            addition = min(limit - given[i], max(1, budget * loads[i] // pool), rest)
            given[i] = given[i] + addition
            rest = rest - addition
    return np.array(given)


def gaussian(stream_key, shape, spread, bound, pieces=(), kind=jnp.bfloat16):
    drawn = jax.random.normal(stream_key, shape, jnp.float32) * spread
    if len(pieces) > 0:
        drawn = level_of(stream_key, shape, pieces, -0.22, 0.18) * drawn
    return jnp.clip(drawn, min=-bound, max=bound).astype(kind)


def setup_inputs(seed: int = 0, part: int = 0) -> dict:
    seeds = jax.random.split(jax.random.key(seed), 7)
    part_splits = jax.random.split(jax.random.fold_in(seeds[6], part), 7)
    tokens = gaussian(part_splits[0], (TOKENS, D), 1.0, 6.0, ((0, 16),))
    expert_ids_keys = jax.random.split(jax.random.fold_in(part_splits[1], 1), TOKENS // TOK_DEV)
    expert_ids_turns = jax.random.permutation(jax.random.fold_in(part_splits[1], 3), TOKENS // TOK_DEV)
    expert_ids = jax.vmap(lambda own, number: assign_block(jax.random.fold_in(part_splits[1], 2), own, number, TOK_DEV, EXPERTS, TOP, CAP, 1))(expert_ids_keys, expert_ids_turns).reshape((TOKENS, TOP))
    gate_probs = jnp.clip(0.099609375 + 0.49804688 * jax.random.uniform(part_splits[2], (TOKENS, TOP), jnp.float32) ** level_of(part_splits[2], (TOKENS, TOP), ((0, 16),), -0.2, 0.2), 0.099609375, 0.59765625).astype(jnp.bfloat16)
    cotangent = gaussian(part_splits[3], (TOKENS, D), 0.25, 1.5, ((0, 16),))
    gate_up = gaussian(seeds[4], (D, EXPERTS, 2 * FF), D ** -0.5, 0.1875, ((1, 4),))
    down_weights = gaussian(seeds[5], (FF, EXPERTS, D), FF ** -0.5, 0.21875, ((1, 4),))
    return {"tokens": tokens, "expert_ids": expert_ids, "gate_probs": gate_probs, "cotangent": cotangent, "gate_up": gate_up, "down_weights": down_weights}


def slot_table(expert_ids, experts, capacity):
    flat_ids = expert_ids.reshape(-1)
    assigned = flat_ids.shape[0]
    onehot = (flat_ids[:, None] == jnp.arange(experts, dtype=jnp.int32)[None, :]).astype(jnp.int32)
    before = jnp.cumsum(onehot, axis=0) - onehot
    slot_index = jnp.sum(before * onehot, axis=1).astype(jnp.int32)
    position = (flat_ids * capacity + slot_index).astype(jnp.int32)
    slot_owner = jnp.full((experts * capacity,), assigned, jnp.int32).at[position].set(jnp.arange(assigned, dtype=jnp.int32))
    return position, slot_owner


def regroup(values):
    return values.reshape(N_EXPERT, EXPERTS, CAP, -1).swapaxes(0, 1).reshape(EXPERTS, N_EXPERT * CAP, -1)


def ungroup(values):
    return values.reshape(EXPERTS, N_EXPERT, CAP, -1).swapaxes(0, 1).reshape(N_EXPERT, EXPERTS * CAP, -1)


def split_rows(values):
    return values.reshape((N_EXPERT, N_REPLICA, TOK_DEV) + values.shape[1:]).swapaxes(0, 1)


def join_rows(values):
    return values.swapaxes(0, 1).reshape((TOKENS,) + values.shape[3:])


def reference(tokens, expert_ids, gate_probs, cotangent, gate_up, down_weights):
    gate_float = gate_up.astype(jnp.float32)
    down_float = down_weights.astype(jnp.float32)

    def one_row(carry, row_data):
        row_tokens, row_ids, row_probs, row_cot = row_data
        position, slot_owner = jax.vmap(lambda choose: slot_table(choose, EXPERTS, CAP))(row_ids)
        zero_rows = jnp.zeros((N_EXPERT, 1, D), jnp.bfloat16)
        padded = jnp.concatenate([row_tokens, zero_rows], axis=1)
        dispatched = jax.vmap(lambda values, owners: values[owners // TOP])(padded, slot_owner)
        grouped = regroup(dispatched)
        pre_act = jnp.einsum("erd,def->erf", grouped.astype(jnp.float32), gate_float)
        gate_part = pre_act[..., :FF]
        up_part = pre_act[..., FF:]
        hidden = (jax.nn.silu(gate_part) * up_part).astype(jnp.bfloat16)
        outputs = jnp.einsum("erf,fed->erd", hidden.astype(jnp.float32), down_float).astype(jnp.bfloat16)
        picked = jax.vmap(lambda values, places: values[places])(ungroup(outputs), position)
        picked = picked.reshape(N_EXPERT, TOK_DEV, TOP, D).astype(jnp.float32)
        probs_float = row_probs.astype(jnp.float32)
        combined = jnp.sum(probs_float[..., None] * picked, axis=2).astype(jnp.bfloat16)
        cot_float = row_cot.astype(jnp.float32)
        prob_gradient = jnp.sum(cot_float[:, :, None, :] * picked, axis=3)
        scaled = (probs_float[..., None] * cot_float[:, :, None, :]).astype(jnp.bfloat16).reshape(N_EXPERT, TOK_DEV * TOP, D)
        scaled = jnp.concatenate([scaled, zero_rows], axis=1)
        cot_slots = regroup(jax.vmap(lambda values, owners: values[owners])(scaled, slot_owner))
        hidden_grad = jnp.einsum("erd,fed->erf", cot_slots.astype(jnp.float32), down_float)
        sigmoid_gate = jax.nn.sigmoid(gate_part)
        pre_gradient = jnp.concatenate([hidden_grad * up_part * sigmoid_gate * (1.0 + gate_part * (1.0 - sigmoid_gate)), hidden_grad * gate_part * sigmoid_gate], axis=-1).astype(jnp.bfloat16)
        input_grads = jnp.einsum("erf,def->erd", pre_gradient.astype(jnp.float32), gate_float).astype(jnp.bfloat16)
        returned = jax.vmap(lambda values, places: values[places])(ungroup(input_grads), position)
        token_gradient = jnp.sum(returned.reshape(N_EXPERT, TOK_DEV, TOP, D).astype(jnp.float32), axis=2).astype(jnp.bfloat16)
        grad_inner = jnp.einsum("erd,erf->def", grouped.astype(jnp.float32), pre_gradient.astype(jnp.float32))
        grad_down = jnp.einsum("erf,erd->fed", hidden.astype(jnp.float32), cot_slots.astype(jnp.float32))
        return (carry[0] + grad_inner, carry[1] + grad_down), (combined, token_gradient, prob_gradient)

    start_sums = (jnp.zeros((D, EXPERTS, 2 * FF), jnp.float32), jnp.zeros((FF, EXPERTS, D), jnp.float32))
    sums, row_outs = lax.scan(one_row, start_sums, (split_rows(tokens), split_rows(expert_ids), split_rows(gate_probs), split_rows(cotangent)))
    combined, token_gradient, prob_gradient = row_outs
    return join_rows(combined), join_rows(token_gradient), join_rows(prob_gradient), sums[0], sums[1]
```

```python
import functools

import jax
import jax.numpy as jnp
from jax import lax
from jax.experimental import pallas as pl
from jax.experimental.pallas import tpu as pltpu
from jax.sharding import PartitionSpec as P

CAP = 64
HALVES = 2
VMEM_LIMIT = 56 * 1024 * 1024
BF = jnp.bfloat16
F32 = jnp.float32


def mm(a, b):
    return jnp.dot(a, b, preferred_element_type=F32)


def mm_t0(a, b):
    return lax.dot_general(a, b, (((0,), (0,)), ((), ())), preferred_element_type=F32)


def mm_t1(a, b):
    return lax.dot_general(a, b, (((1,), (1,)), ((), ())), preferred_element_type=F32)


def full(shape):
    return pl.BlockSpec(shape, lambda e, s: (0,) * len(shape))


def per_expert(shape):
    return pl.BlockSpec((1,) + tuple(shape[1:]), lambda e, s: (e,) + (0,) * (len(shape) - 1))


def params():
    return pltpu.CompilerParams(vmem_limit_bytes=VMEM_LIMIT)


def table_kernel(experts, ids_ref, probs_ref, out_ref):
    count, top = ids_ref.shape
    row = lax.broadcasted_iota(jnp.int32, (count, count), 0)
    col = lax.broadcasted_iota(jnp.int32, (count, count), 1)
    eye = (row == col).astype(F32).astype(BF)
    ids = mm_t0(ids_ref[...].astype(F32).astype(BF), eye)
    probs = mm_t0(probs_ref[...], eye)
    expert = lax.broadcasted_iota(jnp.int32, (experts, count), 0).astype(F32)
    member = jnp.zeros((experts, count), F32)
    weight = jnp.zeros((experts, count), F32)
    for k in range(top):
        hit = ids[k : k + 1, :] == expert
        member = member + hit.astype(F32)
        weight = weight + jnp.where(hit, probs[k : k + 1, :], 0.0)
    earlier = (row < col).astype(F32).astype(BF)
    rank = mm(member.astype(BF), earlier)
    out_ref[:experts, :] = jnp.where(member > 0.0, rank, -1.0).astype(BF)
    out_ref[experts:, :] = weight.astype(BF)


def make_table(ids, probs, experts):
    return pl.pallas_call(
        functools.partial(table_kernel, experts),
        out_shape=jax.ShapeDtypeStruct((2 * experts, ids.shape[0]), BF),
        compiler_params=params(),
    )(ids, probs)


def masks(table, first, local):
    experts, count = table.shape[0] // 2, table.shape[1]
    named = lax.broadcasted_iota(jnp.int32, (CAP, experts), 1)
    pick = jnp.concatenate([(named == first + i).astype(F32) for i in range(local)], axis=0).astype(BF)
    slot = lax.broadcasted_iota(jnp.int32, (CAP, count), 0).astype(F32)
    slot = jnp.concatenate([slot] * local, axis=0)
    hit = mm(pick, table[:experts, :]) == slot
    weight = jnp.where(hit, mm(pick, table[experts:, :]), 0.0)
    return hit.astype(F32), weight


def scatter_slots(dst, values, d, local):
    for i in range(local):
        dst[i, d * CAP : (d + 1) * CAP, :] = values[i * CAP : (i + 1) * CAP, :]


def forward_kernel(n, local, scal, *refs):
    toks, tabs, (wgu, wd), (x_ref, gu_ref, h_ref, o_ref), combs = (
        refs[:n], refs[n : 2 * n], refs[2 * n : 2 * n + 2], refs[2 * n + 2 : 2 * n + 6], refs[2 * n + 6 :],
    )
    e = pl.program_id(0)
    first = scal[0]

    @pl.when(e == 0)
    def _():
        for d in range(n):
            hit, _w = masks(tabs[d][...], first, local)
            scatter_slots(x_ref, mm(hit.astype(BF), toks[d][...]).astype(BF), d, local)

    pre = mm(x_ref[e], wgu[0])
    gu_ref[0] = pre
    middle = pre.shape[-1] // 2
    hidden = (jax.nn.silu(pre[:, :middle]) * pre[:, middle:]).astype(BF)
    h_ref[0] = hidden
    out = mm(hidden, wd[0]).astype(BF)
    for d in range(n):
        o_ref[d, pl.ds(pl.multiple_of(e * CAP, CAP), CAP), :] = out[d * CAP : (d + 1) * CAP, :]

    @pl.when(e == local - 1)
    def _():
        for d in range(n):
            _h, weight = masks(tabs[d][...], first, local)
            combs[d][...] = mm_t0(weight.astype(BF), o_ref[d]).astype(BF)


def forward(scal, toks, tabs, wgu, wd):
    n, (local, width, two_f) = len(toks), wgu.shape
    count, rows, ff = toks[0].shape[0], n * CAP, two_f // 2
    outs = [
        (jax.ShapeDtypeStruct((local, rows, width), BF), full((local, rows, width))),
        (jax.ShapeDtypeStruct((local, rows, two_f), F32), per_expert((local, rows, two_f))),
        (jax.ShapeDtypeStruct((local, rows, ff), BF), per_expert((local, rows, ff))),
        (jax.ShapeDtypeStruct((n, local * CAP, width), BF), full((n, local * CAP, width))),
    ] + [(jax.ShapeDtypeStruct((count, width), BF), full((count, width)))] * n
    res = pl.pallas_call(
        functools.partial(forward_kernel, n, local),
        grid_spec=pltpu.PrefetchScalarGridSpec(
            num_scalar_prefetch=1,
            grid=(local,),
            in_specs=[full(a.shape) for a in (*toks, *tabs)] + [per_expert(wgu.shape), per_expert(wd.shape)],
            out_specs=[o[1] for o in outs],
        ),
        out_shape=[o[0] for o in outs],
        compiler_params=params(),
        cost_estimate=pl.CostEstimate(
            flops=6 * local * rows * width * ff, bytes_accessed=40 << 20, transcendentals=local * rows * ff
        ),
    )(scal, *toks, *tabs, wgu, wd)
    return res[0], res[1], res[2], res[3], list(res[4:])


def act_gradient(pre, hidden_grad):
    middle = pre.shape[-1] // 2
    g, u = pre[:, :middle], pre[:, middle:]
    s = jax.nn.sigmoid(g)
    return jnp.concatenate(
        [hidden_grad * u * s * (1.0 + g * (1.0 - s)), hidden_grad * g * s], axis=-1
    ).astype(BF)


def backward_kernel(n, local, scal, *refs):
    cots, tabs, (gu_ref, o_ref, wgu, wd), (pg_ref, gs_ref) = (
        refs[:n], refs[n : 2 * n], refs[2 * n : 2 * n + 4], refs[2 * n + 4 : 2 * n + 6],
    )
    tokgs, pgms, dx_ref = refs[2 * n + 6 : 3 * n + 6], refs[3 * n + 6 : 4 * n + 6], refs[4 * n + 6]
    e = pl.program_id(0)
    first = scal[0]

    @pl.when(e == 0)
    def _():
        for d in range(n):
            hit, weight = masks(tabs[d][...], first, local)
            slots = mm(hit.astype(BF), cots[d][...])
            scale = jnp.sum(weight, axis=1, keepdims=True)
            scatter_slots(gs_ref, (scale * slots).astype(BF), d, local)
            dots = jnp.sum(slots * o_ref[d].astype(F32), axis=1, keepdims=True)
            spread = hit * dots
            for i in range(local):
                pgms[d][i : i + 1, :] = jnp.sum(spread[i * CAP : (i + 1) * CAP, :], axis=0, keepdims=True)

    hidden_grad = mm_t1(gs_ref[e], wd[0])
    pg = act_gradient(gu_ref[0], hidden_grad)
    pg_ref[0] = pg
    dx = mm_t1(pg, wgu[0]).astype(BF)
    for d in range(n):
        dx_ref[d, pl.ds(pl.multiple_of(e * CAP, CAP), CAP), :] = dx[d * CAP : (d + 1) * CAP, :]

    @pl.when(e == local - 1)
    def _():
        for d in range(n):
            hit, _w = masks(tabs[d][...], first, local)
            tokgs[d][...] = mm_t0(hit.astype(BF), dx_ref[d]).astype(BF)


def backward(scal, cots, tabs, gu, o, wgu, wd):
    n, (local, width, two_f) = len(cots), wgu.shape
    count, rows, ff = cots[0].shape[0], n * CAP, two_f // 2
    outs = (
        [
            (jax.ShapeDtypeStruct((local, rows, two_f), BF), per_expert((local, rows, two_f))),
            (jax.ShapeDtypeStruct((local, rows, width), BF), full((local, rows, width))),
        ]
        + [(jax.ShapeDtypeStruct((count, width), BF), full((count, width)))] * n
        + [(jax.ShapeDtypeStruct((local, count), F32), full((local, count)))] * n
    )
    res = pl.pallas_call(
        functools.partial(backward_kernel, n, local),
        grid_spec=pltpu.PrefetchScalarGridSpec(
            num_scalar_prefetch=1,
            grid=(local,),
            in_specs=[full(a.shape) for a in (*cots, *tabs)]
            + [per_expert(gu.shape), full(o.shape), per_expert(wgu.shape), per_expert(wd.shape)],
            out_specs=[o_[1] for o_ in outs],
            scratch_shapes=[pltpu.VMEM((n, local * CAP, width), BF)],
        ),
        out_shape=[o_[0] for o_ in outs],
        compiler_params=params(),
        cost_estimate=pl.CostEstimate(
            flops=6 * local * rows * width * ff, bytes_accessed=40 << 20, transcendentals=local * rows * ff
        ),
    )(scal, *cots, *tabs, gu, o, wgu, wd)
    return res[0], res[1], list(res[2 : 2 + n]), list(res[2 + n :])


def weight_kernel(n, local, low, experts, scal, *refs):
    toks, cots = refs[:n], refs[n : 2 * n]
    tab_ref, x_ref, h_ref, pg_ref, gs_ref, wgu, wd = refs[2 * n : 2 * n + 7]
    rest = refs[2 * n + 7 :]
    gates, downs = rest[:low], rest[low : 2 * low]
    xo, go, ho, acc_g, acc_d = rest[2 * low :]
    e = pl.program_id(0)
    first, hi, lo = scal[0], scal[1], scal[2]

    @pl.when(e == 0)
    def _():
        for d in range(n):
            hit, weight = masks(tab_ref[d * 2 * experts : (d + 1) * 2 * experts, :], first, local)
            scatter_slots(xo, mm(hit.astype(BF), toks[d][...]).astype(BF), d, local)
            scatter_slots(go, mm(weight.astype(BF), cots[d][...]).astype(BF), d, local)

    pre = mm(xo[e], wgu[0])
    middle = pre.shape[-1] // 2
    ho[...] = (jax.nn.silu(pre[:, :middle]) * pre[:, middle:]).astype(BF)
    pg = act_gradient(pre, mm_t1(go[e], wd[0]))
    half_d, half_f = acc_g.shape[0], acc_d.shape[0]
    cols = pl.ds(pl.multiple_of(hi * half_d, half_d), half_d)
    acc_g[...] = mm_t0(x_ref[0, :, cols], pg_ref[0]) + mm_t0(xo[e, :, cols], pg)
    cols = pl.ds(pl.multiple_of(hi * half_f, half_f), half_f)
    acc_d[...] = mm_t0(h_ref[0, :, cols], gs_ref[0]) + mm_t0(ho[:, cols], go[e])
    for j in range(low):
        block = lax.rem(lo + j, low)
        for acc, dst in ((acc_g, gates[j]), (acc_d, downs[j])):
            size = acc.shape[0] // low
            dst[0] = acc[pl.ds(pl.multiple_of(block * size, size), size), :].astype(dst.dtype)


def weight_gradients(scal, low, toks, cots, tab, x, h, pg, gs, wgu, wd):
    n, (local, width, two_f) = len(toks), wgu.shape
    rows, ff = n * CAP, two_f // 2
    half_d, half_f = width // HALVES, ff // HALVES
    outs = []
    for size, lanes in ((half_d // low, two_f), (half_f // low, width)):
        for j in range(low):
            shape = (local, size, lanes)
            outs.append((jax.ShapeDtypeStruct(shape, BF if j else F32), per_expert(shape)))
    res = pl.pallas_call(
        functools.partial(weight_kernel, n, local, low, tab.shape[0] // (2 * n)),
        grid_spec=pltpu.PrefetchScalarGridSpec(
            num_scalar_prefetch=1,
            grid=(local,),
            in_specs=[full(a.shape) for a in (*toks, *cots, tab)]
            + [per_expert(a.shape) for a in (x, h, pg, gs, wgu, wd)],
            out_specs=[o[1] for o in outs],
            scratch_shapes=[
                pltpu.VMEM((local, rows, width), BF),
                pltpu.VMEM((local, rows, width), BF),
                pltpu.VMEM((rows, ff), BF),
                pltpu.VMEM((half_d, two_f), F32),
                pltpu.VMEM((half_f, width), F32),
            ],
        ),
        out_shape=[o[0] for o in outs],
        compiler_params=params(),
        cost_estimate=pl.CostEstimate(
            flops=12 * local * rows * width * ff, bytes_accessed=50 << 20, transcendentals=local * rows * ff
        ),
    )(scal, *toks, *cots, tab, x, h, pg, gs, wgu, wd)
    return res[:low], res[low:]


def on_device(n, replicas, tokens, expert_ids, gate_probs, cotangent, gate_up, down_weights):
    local = gate_up.shape[1]
    experts = n * local
    low = replicas // HALVES
    z, r = lax.axis_index("expert"), lax.axis_index("replica")
    scal = jnp.stack([z * local, r // low, r % low]).astype(jnp.int32)
    ring = [(i, (i + 1) % n) for i in range(n)]
    across = [(i, (i + low) % replicas) for i in range(replicas)]

    table = make_table(expert_ids, gate_probs, experts)
    toks, tabs, cots = [tokens], [table], [cotangent]
    for _ in range(n - 1):
        toks.append(lax.ppermute(toks[-1], "expert", ring))
        tabs.append(lax.ppermute(tabs[-1], "expert", ring))
        cots.append(lax.ppermute(cots[-1], "expert", ring))
    other_toks = [lax.ppermute(t, "replica", across) for t in toks]
    other_cots = [lax.ppermute(t, "replica", across) for t in cots]
    other_tab = lax.ppermute(jnp.concatenate(tabs, axis=0), "replica", across)

    wgu = jnp.transpose(gate_up, (1, 0, 2))
    wd = jnp.transpose(down_weights, (1, 0, 2))
    x, gu, h, o, combs = forward(scal, toks, tabs, wgu, wd)
    pg, gs, tokgs, pgms = backward(scal, cots, tabs, gu, o, wgu, wd)

    def ring_sum(parts):
        total = parts[1]
        for d in range(2, n + 1):
            total = lax.ppermute(total, "expert", ring)
            total = (total.astype(F32) + parts[d % n].astype(F32)).astype(BF)
        return total

    combined = ring_sum(combs)
    token_gradient = ring_sum(tokgs)
    gates, downs = weight_gradients(scal, low, other_toks, other_cots, other_tab, x, h, pg, gs, wgu, wd)
    sums = []
    for blocks in (gates, downs):
        total = blocks[0]
        for j in range(1, low):
            step = [(i, i // low * low + (i % low + j) % low) for i in range(replicas)]
            total = total + lax.ppermute(blocks[j], "replica", step).astype(F32)
        sums.append(jnp.transpose(total, (1, 0, 2)))

    found = [pgms[0]]
    for d in range(1, n):
        found.append(lax.ppermute(pgms[d], "expert", [(i, (i - d) % n) for i in range(n)]))
    prob_gradient = jnp.zeros(expert_ids.shape, F32)
    for d in range(n):
        for i in range(local):
            name = lax.rem(z + d, n) * local + i
            prob_gradient = prob_gradient + jnp.where(expert_ids == name, found[d][i][:, None], 0.0)
    return (combined, token_gradient, prob_gradient, sums[0], sums[1])


def solution(mesh):
    rows = P(("groups", "expert", "replica"), None)
    weights = P(None, "expert", None)
    shares = P(("groups", "replica"), "expert", None)
    return jax.shard_map(
        functools.partial(on_device, mesh.shape["expert"], mesh.shape["replica"]),
        mesh=mesh,
        in_specs=(rows, rows, rows, rows, weights, weights),
        out_specs=(rows, rows, rows, shares, shares),
        check_vma=False,
    )
```

```python
import functools

import jax
import jax.numpy as jnp
from jax import lax
from jax.experimental import pallas as pl
from jax.experimental.pallas import tpu as pltpu
from jax.sharding import PartitionSpec as P

CAP = 64
HALVES = 2
VMEM_LIMIT = 56 * 1024 * 1024
BF = jnp.bfloat16
F32 = jnp.float32


def mm(a, b):
    return jnp.dot(a, b, preferred_element_type=F32)


def mm_t0(a, b):
    return lax.dot_general(a, b, (((0,), (0,)), ((), ())), preferred_element_type=F32)


def mm_t1(a, b):
    return lax.dot_general(a, b, (((1,), (1,)), ((), ())), preferred_element_type=F32)


def full(shape):
    return pl.BlockSpec(shape, lambda e, s: (0,) * len(shape))


def per_expert(shape):
    return pl.BlockSpec((1,) + tuple(shape[1:]), lambda e, s: (e,) + (0,) * (len(shape) - 1))


def params():
    return pltpu.CompilerParams(vmem_limit_bytes=VMEM_LIMIT)


def pack_kernel(ids_ref, probs_ref, tok_ref, cot_ref, out_ref):
    top, count = ids_ref.shape
    experts = out_ref.shape[0] - 2 * count
    out_ref[:count, :] = tok_ref[...]
    out_ref[count : 2 * count, :] = cot_ref[...]
    ids, probs = ids_ref[...], probs_ref[...].astype(F32)
    expert = lax.broadcasted_iota(jnp.int32, (experts, count), 0)
    member = jnp.zeros((experts, count), F32)
    weight = jnp.zeros((experts, count), F32)
    for k in range(top):
        hit = ids[k : k + 1, :] == expert
        member = member + hit.astype(F32)
        weight = weight + jnp.where(hit, probs[k : k + 1, :], 0.0)
    row = lax.broadcasted_iota(jnp.int32, (count, count), 0)
    col = lax.broadcasted_iota(jnp.int32, (count, count), 1)
    rank = mm(member.astype(BF), (row < col).astype(F32).astype(BF))
    slot = jnp.where(member > 0.0, rank, -1.0)
    rest = jnp.zeros((experts, out_ref.shape[1] - 2 * count), F32)
    out_ref[2 * count :, :] = jnp.concatenate([slot, weight, rest], axis=1).astype(BF)


def pack(ids, probs, tokens, cot, experts):
    count, width = tokens.shape
    return pl.pallas_call(
        pack_kernel,
        out_shape=jax.ShapeDtypeStruct((2 * count + experts, width), BF),
        compiler_params=pltpu.CompilerParams(vmem_limit_bytes=8 * 1024 * 1024),
    )(ids.T, probs.T, tokens, cot)


def masks(pay, count, first, local):
    experts = pay.shape[0] - 2 * count
    named = lax.broadcasted_iota(jnp.int32, (CAP, experts), 1)
    pick = jnp.concatenate([(named == first + i).astype(F32) for i in range(local)], axis=0).astype(BF)
    slot = lax.broadcasted_iota(jnp.int32, (CAP, count), 0).astype(F32)
    slot = jnp.concatenate([slot] * local, axis=0)
    hit = mm(pick, pay[2 * count :, :count]) == slot
    weight = jnp.where(hit, mm(pick, pay[2 * count :, count : 2 * count]), 0.0)
    return hit.astype(F32), weight


def scatter_slots(dst, values, d, local):
    for i in range(local):
        dst[i, d * CAP : (d + 1) * CAP, :] = values[i * CAP : (i + 1) * CAP, :]


def act_gradient(pre, hidden_grad):
    middle = pre.shape[-1] // 2
    g, u = pre[:, :middle], pre[:, middle:]
    s = jax.nn.sigmoid(g)
    return jnp.concatenate(
        [hidden_grad * u * s * (1.0 + g * (1.0 - s)), hidden_grad * g * s], axis=-1
    ).astype(BF)


def stage_kernel(m, local, count, own, after, scal, *refs):
    pays, (wgu, wd) = refs[:m], refs[m : m + 2]
    refs = refs[m + 2 + after :]
    x_ref, h_ref, pg_ref, gs_ref = refs[:4]
    refs = refs[4:]
    if own:
        sums, (hit_s, wt_s, cs, o_s, dx_s, dots_s) = refs[:m], refs[m:]
    e = pl.program_id(0)
    here = pl.ds(pl.multiple_of(e * CAP, CAP), CAP)

    @pl.when(e == 0)
    def _():
        for d in range(m):
            hit, weight = masks(pays[d], count, scal[0], local)
            hit_b = hit.astype(BF)
            scatter_slots(x_ref, mm(hit_b, pays[d][:count, :]).astype(BF), d, local)
            if own:
                hit_s[d] = hit_b
                wt_s[d] = weight.astype(BF)
                slots = mm(hit_b, pays[d][count : 2 * count, :])
                scatter_slots(cs, slots.astype(BF), d, local)
                slots = jnp.sum(weight, axis=1, keepdims=True) * slots
            else:
                slots = mm(weight.astype(BF), pays[d][count : 2 * count, :])
            scatter_slots(gs_ref, slots.astype(BF), d, local)

    pre = mm(x_ref[e], wgu[0])
    middle = pre.shape[-1] // 2
    hidden = (jax.nn.silu(pre[:, :middle]) * pre[:, middle:]).astype(BF)
    h_ref[0] = hidden
    pg = act_gradient(pre, mm_t1(gs_ref[e], wd[0]))
    pg_ref[0] = pg
    if own:
        out = mm(hidden, wd[0]).astype(BF)
        dots = jnp.sum(cs[e].astype(F32) * out.astype(F32), axis=1, keepdims=True)
        dx = mm_t1(pg, wgu[0]).astype(BF)
        for d in range(m):
            part = slice(d * CAP, (d + 1) * CAP)
            o_s[d, here, :] = out[part]
            dx_s[d, here, :] = dx[part]
            spread = hit_s[d, here, :].astype(F32) * dots[part]
            dots_s[d, pl.ds(e, 1), :] = jnp.sum(spread, axis=0, keepdims=True)

        @pl.when(e == local - 1)
        def _():
            for d in range(m):
                sums[d][:count, :] = mm_t0(wt_s[d], o_s[d]).astype(BF)
                sums[d][count : 2 * count, :] = mm_t0(hit_s[d], dx_s[d]).astype(BF)
                experts, width = sums[d].shape[0] - 2 * count, sums[d].shape[1]
                row = lax.broadcasted_iota(jnp.int32, (experts, count), 0)
                dots = jnp.zeros((experts, count), F32)
                for i in range(local):
                    dots = dots + jnp.where(row == scal[0] + i, dots_s[d, i : i + 1, :], 0.0)
                upper = dots.astype(BF).astype(F32)
                rest = jnp.zeros((experts, width - 2 * count), F32)
                sums[d][2 * count :, :] = jnp.concatenate([upper, dots - upper, rest], axis=1).astype(BF)


def stage(scal, pays, count, wgu, wd, own, after=()):
    m, (local, width, two_f) = len(pays), wgu.shape
    rows, ff = m * CAP, two_f // 2
    outs = [
        (jax.ShapeDtypeStruct((local, rows, width), BF), full((local, rows, width))),
        (jax.ShapeDtypeStruct((local, rows, ff), BF), per_expert((local, rows, ff))),
        (jax.ShapeDtypeStruct((local, rows, two_f), BF), per_expert((local, rows, two_f))),
        (jax.ShapeDtypeStruct((local, rows, width), BF), full((local, rows, width))),
    ]
    scratch = []
    if own:
        outs += [(jax.ShapeDtypeStruct(a.shape, BF), full(a.shape)) for a in pays]
        scratch = [
            pltpu.VMEM((m, local * CAP, count), BF),
            pltpu.VMEM((m, local * CAP, count), BF),
            pltpu.VMEM((local, rows, width), BF),
            pltpu.VMEM((m, local * CAP, width), BF),
            pltpu.VMEM((m, local * CAP, width), BF),
            pltpu.VMEM((m, local, count), F32),
        ]
    res = pl.pallas_call(
        functools.partial(stage_kernel, m, local, count, own, len(after)),
        grid_spec=pltpu.PrefetchScalarGridSpec(
            num_scalar_prefetch=1,
            grid=(local,),
            in_specs=[full(a.shape) for a in pays]
            + [per_expert(wgu.shape), per_expert(wd.shape)]
            + [pl.BlockSpec(memory_space=pl.ANY)] * len(after),
            out_specs=[o[1] for o in outs],
            scratch_shapes=scratch,
        ),
        out_shape=[o[0] for o in outs],
        compiler_params=params(),
        cost_estimate=pl.CostEstimate(
            flops=(48 if own else 34) * local * rows * width * ff, bytes_accessed=24 << 20, transcendentals=local * rows * ff
        ),
    )(scal, *pays, wgu, wd, *after)
    return res[:4], list(res[4:])


def send_kernel(parts, low, scal, *refs):
    xs, hs, pgs, gss = (refs[k * parts : (k + 1) * parts] for k in range(4))
    gates, downs, own_down, acc_d = refs[4 * parts : 4 * parts + low - 1], refs[4 * parts + low - 1 : -2], refs[-2], refs[-1]
    lo = scal[2]
    pg = jnp.concatenate([p[0] for p in pgs], axis=0)
    size = xs[0].shape[-1] // low
    for j in range(1, low):
        cols = pl.ds(pl.multiple_of(lax.rem(lo + j, low) * size, size), size)
        gates[j - 1][0] = mm_t0(jnp.concatenate([x[0, :, cols] for x in xs], axis=0), pg).astype(BF)
    h = jnp.concatenate([h_[0] for h_ in hs], axis=0)
    acc_d[...] = mm_t0(h, jnp.concatenate([g[0] for g in gss], axis=0))
    size = acc_d.shape[0] // low
    for j in range(low):
        block = acc_d[pl.ds(pl.multiple_of(lax.rem(lo + j, low) * size, size), size), :]
        if j:
            downs[j - 1][0] = block.astype(BF)
        else:
            own_down[0] = block


def send_blocks(scal, low, stages, start, local, after=()):
    xs, hs, pgs, gss = zip(*stages)
    width = xs[0].shape[-1]
    ff = hs[0].shape[-1]
    half_d, half_f = width // HALVES, ff // HALVES
    of_half = lambda a, size: pl.BlockSpec((1, a.shape[1], size), lambda e, s: (e + start, 0, s[1]))
    whole = lambda a: pl.BlockSpec((1,) + a.shape[1:], lambda e, s: (e + start, 0, 0))
    gate_shape, down_shape = (local, half_d // low, 2 * ff), (local, half_f // low, width)
    outs = [jax.ShapeDtypeStruct(gate_shape, BF)] * (low - 1)
    outs += [jax.ShapeDtypeStruct(down_shape, BF)] * (low - 1) + [jax.ShapeDtypeStruct(down_shape, F32)]
    k = len(after)
    body = functools.partial(send_kernel, len(stages), low)
    res = pl.pallas_call(
        lambda s, *refs: body(s, *refs[k:]),
        grid_spec=pltpu.PrefetchScalarGridSpec(
            num_scalar_prefetch=1,
            grid=(local,),
            in_specs=[pl.BlockSpec(memory_space=pl.ANY)] * k
            + [of_half(x, half_d) for x in xs]
            + [of_half(h, half_f) for h in hs]
            + [whole(a) for a in (*pgs, *gss)],
            out_specs=[per_expert(o.shape) for o in outs],
            scratch_shapes=[pltpu.VMEM((half_f, width), F32)],
        ),
        out_shape=outs,
        compiler_params=params(),
        cost_estimate=pl.CostEstimate(
            flops=36 * local * xs[0].shape[1] * width * ff, bytes_accessed=24 << 20, transcendentals=0
        ),
    )(scal, *after, *xs, *hs, *pgs, *gss)
    return res[: low - 1], res[low - 1 : 2 * low - 2], res[-1]


def keep_kernel(parts, pieces, low, scal, *refs):
    xs, pgs, refs = refs[:parts], refs[parts : 2 * parts], refs[2 * parts :]
    gate_ref, down_ref = refs[-2:]
    each = gate_ref.shape[1] // pieces
    got = [refs[k * (2 * low - 1) : (k + 1) * (2 * low - 1)] for k in range(pieces)]
    size = xs[0].shape[-1] // low
    cols = pl.ds(pl.multiple_of(scal[2] * size, size), size)
    for e in range(gate_ref.shape[1]):
        total = mm_t0(
            jnp.concatenate([x[e, :, cols] for x in xs], axis=0), jnp.concatenate([p[e] for p in pgs], axis=0)
        )
        arrived = got[e // each]
        gate_ref[:, e, :] = total + sum(g[e % each].astype(F32) for g in arrived[: low - 1])
        down_ref[:, e, :] = arrived[-1][e % each] + sum(g[e % each].astype(F32) for g in arrived[low - 1 : -1])


def keep_blocks(scal, low, stages, pieces, after=()):
    xs, _, pgs, _ = zip(*stages)
    local, rows, width = xs[0].shape
    two_f = pgs[0].shape[-1]
    half_d = width // HALVES
    steps = 4
    lanes = lambda a: pl.BlockSpec(a.shape[:-1] + (a.shape[-1] // steps,), lambda c, s: (0, 0, c))
    outs = [
        jax.ShapeDtypeStruct((half_d // low, local, two_f), F32),
        jax.ShapeDtypeStruct((pieces[0][-1].shape[1], local, width), F32),
    ]
    k = len(after)
    body = functools.partial(keep_kernel, len(stages), len(pieces), low)
    arrived = [a for piece in pieces for a in piece]
    return pl.pallas_call(
        lambda s, *refs: body(s, *refs[k:]),
        grid_spec=pltpu.PrefetchScalarGridSpec(
            num_scalar_prefetch=1,
            grid=(steps,),
            in_specs=[pl.BlockSpec(memory_space=pl.ANY)] * k
            + [pl.BlockSpec((local, rows, half_d), lambda c, s: (0, 0, s[1]))] * len(xs)
            + [lanes(a) for a in (*pgs, *arrived)],
            out_specs=[lanes(o) for o in outs],
        ),
        out_shape=outs,
        compiler_params=params(),
        cost_estimate=pl.CostEstimate(
            flops=16 * local * rows * width * two_f, bytes_accessed=24 << 20, transcendentals=0
        ),
    )(scal, *after, *xs, *pgs, *arrived)


def on_device(n, replicas, tokens, expert_ids, gate_probs, cotangent, gate_up, down_weights):
    local, count = gate_up.shape[1], tokens.shape[0]
    low = replicas // HALVES
    z, r = lax.axis_index("expert"), lax.axis_index("replica")
    scal = jnp.stack([z * local, r // low, r % low]).astype(jnp.int32)
    ring = [(i, (i + 1) % n) for i in range(n)]
    across = [(i, (i + low) % replicas) for i in range(replicas)]

    pays = [pack(expert_ids, gate_probs, tokens, cotangent, n * local)]
    others = []
    wgu = jnp.transpose(gate_up, (1, 0, 2))
    wd = jnp.transpose(down_weights, (1, 0, 2))
    for d in range(n):
        others.append(lax.ppermute(pays[d], "replica", across))
        if d < n - 1:
            pays.append(lax.ppermute(pays[d], "expert", ring))
            if d == 0:
                pays[1], others[0], wgu, wd = lax.optimization_barrier((pays[1], others[0], wgu, wd))
    near = n // 2
    own_a, sums_a = stage(scal, pays[:near], count, wgu, wd, True)
    other_a, _ = stage(scal, others[:near], count, wgu, wd, False, (sums_a[0], pays[near]))
    own_b, sums_b = stage(scal, pays[near:], count, wgu, wd, True, (other_a[3],))
    sums = sums_a + sums_b

    def add(got, mine):
        return (got.astype(F32) + mine.astype(F32)).astype(BF)

    totals = [sums[1]]
    for d in range(2, n):
        totals.append(add(lax.ppermute(totals[-1], "expert", ring), sums[d]))
    other_b, _ = stage(scal, others[near:], count, wgu, wd, False, (totals[n // 2 - 1],))
    stages = (own_a, other_a, own_b, other_b)
    steps = [[(i, i // low * low + (i % low + j) % low) for i in range(replicas)] for j in range(1, low)]
    pieces, before = [], ()
    for start in range(0, local, -(-local // 2)):
        gates, downs, own_down = send_blocks(scal, low, stages, start, -(-local // 2), before)
        gates = [lax.ppermute(b, "replica", s) for b, s in zip(gates, steps)]
        downs = [lax.ppermute(b, "replica", s) for b, s in zip(downs, steps)]
        pieces.append((*gates, *downs, own_down))
        before = (totals[-1],)
    arrived = lax.ppermute(totals[-1], "expert", ring)
    gate_up_gradient, down_gradient = keep_blocks(scal, low, stages, pieces)
    arrived, gate_up_gradient, down_gradient = lax.optimization_barrier((arrived, gate_up_gradient, down_gradient))
    combined, token_gradient = add(arrived[:count], sums[0][:count]), add(arrived[count : 2 * count], sums[0][count : 2 * count])
    dots = arrived[2 * count :, : 2 * count].astype(F32) + sums[0][2 * count :, : 2 * count].astype(F32)
    dots = dots[:, :count] + dots[:, count:]
    named = expert_ids.T[:, None, :] == jnp.arange(n * local, dtype=jnp.int32)[None, :, None]
    prob_gradient = jnp.sum(jnp.where(named, dots[None], 0.0), axis=1).T
    return (combined, token_gradient, prob_gradient, gate_up_gradient, down_gradient)


def solution(mesh):
    rows = P(("groups", "expert", "replica"), None)
    weights = P(None, "expert", None)
    shares = P(("groups", "replica"), "expert", None)
    return jax.shard_map(
        functools.partial(on_device, mesh.shape["expert"], mesh.shape["replica"]),
        mesh=mesh,
        in_specs=(rows, rows, rows, rows, weights, weights),
        out_specs=(rows, rows, rows, shares, shares),
        check_vma=False,
    )
```

```python
import functools

import jax
import jax.numpy as jnp
from jax import lax
from jax.experimental import pallas as pl
from jax.experimental.pallas import tpu as pltpu
from jax.sharding import PartitionSpec as P

CAP = 64
HALVES = 2
EARLY_VMEM = 34 * 1024 * 1024
STAGE_VMEM = 34 * 1024 * 1024
SHARE_VMEM = 16 * 1024 * 1024
BF = jnp.bfloat16
F32 = jnp.float32


def mm(a, b):
    return jnp.dot(a, b, preferred_element_type=F32)


def mm_t0(a, b):
    return lax.dot_general(a, b, (((0,), (0,)), ((), ())), preferred_element_type=F32)


def mm_t1(a, b):
    return lax.dot_general(a, b, (((1,), (1,)), ((), ())), preferred_element_type=F32)


def full(shape):
    return pl.BlockSpec(shape, lambda e, s: (0,) * len(shape))


def per_expert(shape):
    return pl.BlockSpec((1,) + tuple(shape[1:]), lambda e, s: (e,) + (0,) * (len(shape) - 1))


def pack_kernel(ids_ref, probs_ref, tok_ref, cot_ref, out_ref):
    top, count = ids_ref.shape
    experts = out_ref.shape[0] - 2 * count
    out_ref[:count, :] = tok_ref[...]
    out_ref[count : 2 * count, :] = cot_ref[...]
    ids, probs = ids_ref[...], probs_ref[...].astype(F32)
    expert = lax.broadcasted_iota(jnp.int32, (experts, count), 0)
    member = jnp.zeros((experts, count), F32)
    weight = jnp.zeros((experts, count), F32)
    for k in range(top):
        hit = ids[k : k + 1, :] == expert
        member = member + hit.astype(F32)
        weight = weight + jnp.where(hit, probs[k : k + 1, :], 0.0)
    row = lax.broadcasted_iota(jnp.int32, (count, count), 0)
    col = lax.broadcasted_iota(jnp.int32, (count, count), 1)
    rank = mm(member.astype(BF), (row < col).astype(F32).astype(BF))
    slot = jnp.where(member > 0.0, rank, -1.0)
    rest = jnp.zeros((experts, out_ref.shape[1] - 2 * count), F32)
    out_ref[2 * count :, :] = jnp.concatenate([slot, weight, rest], axis=1).astype(BF)


def pack(ids, probs, tokens, cot, experts):
    count, width = tokens.shape
    return pl.pallas_call(
        pack_kernel,
        out_shape=jax.ShapeDtypeStruct((2 * count + experts, width), BF),
        compiler_params=pltpu.CompilerParams(vmem_limit_bytes=8 * 1024 * 1024),
    )(ids.T, probs.T, tokens, cot)


def masks(pay, count, first, local):
    experts = pay.shape[0] - 2 * count
    named = lax.broadcasted_iota(jnp.int32, (CAP, experts), 1)
    pick = jnp.concatenate([(named == first + i).astype(F32) for i in range(local)], axis=0).astype(BF)
    slot = lax.broadcasted_iota(jnp.int32, (CAP, count), 0).astype(F32)
    slot = jnp.concatenate([slot] * local, axis=0)
    hit = mm(pick, pay[2 * count :, :count]) == slot
    weight = jnp.where(hit, mm(pick, pay[2 * count :, count : 2 * count]), 0.0)
    return hit.astype(F32), weight


def scatter_slots(dst, values, d, local):
    for i in range(local):
        dst[i, d * CAP : (d + 1) * CAP, :] = values[i * CAP : (i + 1) * CAP, :]


def act_gradient(pre, hidden_grad):
    middle = pre.shape[-1] // 2
    g, u = pre[:, :middle], pre[:, middle:]
    s = jax.nn.sigmoid(g)
    return jnp.concatenate(
        [hidden_grad * u * s * (1.0 + g * (1.0 - s)), hidden_grad * g * s], axis=-1
    ).astype(BF)


def stage_kernel(m, own, local, count, after, scal, *refs):
    pays, (wgu, wd) = refs[:m], refs[m : m + 2]
    refs = refs[m + 2 + after :]
    x_ref, h_ref, pg_ref, gs_ref = refs[:4]
    sums, refs = refs[4 : 4 + own], refs[4 + own :]
    xs, hs = refs[:2]
    if own:
        hit_s, wt_s, cs, o_s, dx_s, dots_s = refs[2:]
    e = pl.program_id(0)
    here = pl.ds(pl.multiple_of(e * CAP, CAP), CAP)

    @pl.when(e == 0)
    def _():
        for d in range(m):
            hit, weight = masks(pays[d], count, scal[0], local)
            hit_b = hit.astype(BF)
            scatter_slots(xs, mm(hit_b, pays[d][:count, :]).astype(BF), d, local)
            if d < own:
                hit_s[d] = hit_b
                wt_s[d] = weight.astype(BF)
                slots = mm(hit_b, pays[d][count : 2 * count, :])
                scatter_slots(cs, slots.astype(BF), d, local)
                slots = jnp.sum(weight, axis=1, keepdims=True) * slots
            else:
                slots = mm(weight.astype(BF), pays[d][count : 2 * count, :])
            scatter_slots(gs_ref, slots.astype(BF), d, local)

    half_d, half_f = x_ref.shape[-1], h_ref.shape[-1]
    x_ref[0] = xs[e, :, pl.ds(pl.multiple_of(scal[1] * half_d, half_d), half_d)]
    pre = mm(xs[e], wgu[0])
    middle = pre.shape[-1] // 2
    hidden = (jax.nn.silu(pre[:, :middle]) * pre[:, middle:]).astype(BF)
    hs[...] = hidden
    h_ref[0] = hs[:, pl.ds(pl.multiple_of(scal[1] * half_f, half_f), half_f)]
    pg = act_gradient(pre, mm_t1(gs_ref[e], wd[0]))
    pg_ref[0] = pg
    if own:
        out = mm(hidden[: own * CAP], wd[0]).astype(BF)
        dots = jnp.sum(cs[e].astype(F32) * out.astype(F32), axis=1, keepdims=True)
        dx = mm_t1(pg[: own * CAP], wgu[0]).astype(BF)
        for d in range(own):
            part = slice(d * CAP, (d + 1) * CAP)
            o_s[d, here, :] = out[part]
            dx_s[d, here, :] = dx[part]
            spread = hit_s[d, here, :].astype(F32) * dots[part]
            dots_s[d, pl.ds(e, 1), :] = jnp.sum(spread, axis=0, keepdims=True)

        @pl.when(e == local - 1)
        def _():
            for d in range(own):
                sums[d][:count, :] = mm_t0(wt_s[d], o_s[d]).astype(BF)
                sums[d][count : 2 * count, :] = mm_t0(hit_s[d], dx_s[d]).astype(BF)
                experts, width = sums[d].shape[0] - 2 * count, sums[d].shape[1]
                row = lax.broadcasted_iota(jnp.int32, (experts, count), 0)
                dots = jnp.zeros((experts, count), F32)
                for i in range(local):
                    dots = dots + jnp.where(row == scal[0] + i, dots_s[d, i : i + 1, :], 0.0)
                upper = dots.astype(BF).astype(F32)
                rest = jnp.zeros((experts, width - 2 * count), F32)
                sums[d][2 * count :, :] = jnp.concatenate([upper, dots - upper, rest], axis=1).astype(BF)


def stage(scal, limit, mine, others, count, wgu, wd, after=()):
    pays = (*mine, *others)
    m, own, (local, width, two_f) = len(pays), len(mine), wgu.shape
    rows, ff = m * CAP, two_f // 2
    outs = [
        (jax.ShapeDtypeStruct((local, rows, width // HALVES), BF), per_expert((local, rows, width // HALVES))),
        (jax.ShapeDtypeStruct((local, rows, ff // HALVES), BF), per_expert((local, rows, ff // HALVES))),
        (jax.ShapeDtypeStruct((local, rows, two_f), BF), per_expert((local, rows, two_f))),
        (jax.ShapeDtypeStruct((local, rows, width), BF), full((local, rows, width))),
    ]
    outs += [(jax.ShapeDtypeStruct(a.shape, BF), full(a.shape)) for a in mine]
    scratch = [pltpu.VMEM((local, rows, width), BF), pltpu.VMEM((rows, ff), BF)]
    if own:
        scratch += [
            pltpu.VMEM((own, local * CAP, count), BF),
            pltpu.VMEM((own, local * CAP, count), BF),
            pltpu.VMEM((local, own * CAP, width), BF),
            pltpu.VMEM((own, local * CAP, width), BF),
            pltpu.VMEM((own, local * CAP, width), BF),
            pltpu.VMEM((own, local, count), F32),
        ]
    res = pl.pallas_call(
        functools.partial(stage_kernel, m, own, local, count, len(after)),
        grid_spec=pltpu.PrefetchScalarGridSpec(
            num_scalar_prefetch=1,
            grid=(local,),
            in_specs=[full(a.shape) for a in pays]
            + [per_expert(wgu.shape), per_expert(wd.shape)]
            + [pl.BlockSpec(memory_space=pl.ANY)] * len(after),
            out_specs=[o[1] for o in outs],
            scratch_shapes=scratch,
        ),
        out_shape=[o[0] for o in outs],
        compiler_params=pltpu.CompilerParams(vmem_limit_bytes=limit),
        cost_estimate=pl.CostEstimate(
            flops=(14 if own else 7) * 1000 * 1000 * 1000, bytes_accessed=24 << 20, transcendentals=local * rows * ff
        ),
    )(scal, *pays, wgu, wd, *after)
    return res[:4], list(res[4:])


def send_kernel(parts, low, scal, *refs):
    xs, hs, pgs, gss = (refs[k * parts : (k + 1) * parts] for k in range(4))
    gates, downs, own_down, acc_d = refs[4 * parts : 4 * parts + low - 1], refs[4 * parts + low - 1 : -2], refs[-2], refs[-1]
    lo = scal[2]
    pg = jnp.concatenate([p[0] for p in pgs], axis=0)
    size = xs[0].shape[-1] // low
    for j in range(1, low):
        cols = pl.ds(pl.multiple_of(lax.rem(lo + j, low) * size, size), size)
        gates[j - 1][0] = mm_t0(jnp.concatenate([x[0, :, cols] for x in xs], axis=0), pg).astype(BF)
    h = jnp.concatenate([h_[0] for h_ in hs], axis=0)
    acc_d[...] = mm_t0(h, jnp.concatenate([g[0] for g in gss], axis=0))
    size = acc_d.shape[0] // low
    for j in range(low):
        block = acc_d[pl.ds(pl.multiple_of(lax.rem(lo + j, low) * size, size), size), :]
        if j:
            downs[j - 1][0] = block.astype(BF)
        else:
            own_down[0] = block


def send_blocks(scal, low, stages, start, local, after=()):
    xs, hs, pgs, gss = zip(*stages)
    width, ff = gss[0].shape[-1], pgs[0].shape[-1] // 2
    half_d, half_f = xs[0].shape[-1], hs[0].shape[-1]
    whole = lambda a: pl.BlockSpec((1,) + a.shape[1:], lambda e, s: (e + start, 0, 0))
    gate_shape, down_shape = (local, half_d // low, 2 * ff), (local, half_f // low, width)
    outs = [jax.ShapeDtypeStruct(gate_shape, BF)] * (low - 1)
    outs += [jax.ShapeDtypeStruct(down_shape, BF)] * (low - 1) + [jax.ShapeDtypeStruct(down_shape, F32)]
    k = len(after)
    body = functools.partial(send_kernel, len(stages), low)
    res = pl.pallas_call(
        lambda s, *refs: body(s, *refs[k:]),
        grid_spec=pltpu.PrefetchScalarGridSpec(
            num_scalar_prefetch=1,
            grid=(local,),
            in_specs=[pl.BlockSpec(memory_space=pl.ANY)] * k
            + [whole(a) for a in (*xs, *hs, *pgs, *gss)],
            out_specs=[per_expert(o.shape) for o in outs],
            scratch_shapes=[pltpu.VMEM((half_f, width), F32)],
        ),
        out_shape=outs,
        compiler_params=pltpu.CompilerParams(vmem_limit_bytes=SHARE_VMEM),
        cost_estimate=pl.CostEstimate(
            flops=4 * 1000 * 1000 * 1000, bytes_accessed=24 << 20, transcendentals=0
        ),
    )(scal, *after, *xs, *hs, *pgs, *gss)
    return res[: low - 1], res[low - 1 : 2 * low - 2], res[-1]


def keep_kernel(parts, pieces, low, scal, *refs):
    xs, pgs, refs = refs[:parts], refs[parts : 2 * parts], refs[2 * parts :]
    gate_ref, down_ref = refs[-2:]
    each = gate_ref.shape[1] // pieces
    got = [refs[k * (2 * low - 1) : (k + 1) * (2 * low - 1)] for k in range(pieces)]
    size = xs[0].shape[-1] // low
    cols = pl.ds(pl.multiple_of(scal[2] * size, size), size)
    for e in range(gate_ref.shape[1]):
        total = mm_t0(
            jnp.concatenate([x[e, :, cols] for x in xs], axis=0), jnp.concatenate([p[e] for p in pgs], axis=0)
        )
        arrived = got[e // each]
        gate_ref[:, e, :] = total + sum(g[e % each].astype(F32) for g in arrived[: low - 1])
        down_ref[:, e, :] = arrived[-1][e % each] + sum(g[e % each].astype(F32) for g in arrived[low - 1 : -1])


def keep_blocks(scal, low, stages, pieces, after=()):
    xs, _, pgs, _ = zip(*stages)
    local, rows, half_d = xs[0].shape
    two_f, width = pgs[0].shape[-1], half_d * HALVES
    steps = 4
    lanes = lambda a: pl.BlockSpec(a.shape[:-1] + (a.shape[-1] // steps,), lambda c, s: (0, 0, c))
    outs = [
        jax.ShapeDtypeStruct((half_d // low, local, two_f), F32),
        jax.ShapeDtypeStruct((pieces[0][-1].shape[1], local, width), F32),
    ]
    k = len(after)
    body = functools.partial(keep_kernel, len(stages), len(pieces), low)
    arrived = [a for piece in pieces for a in piece]
    return pl.pallas_call(
        lambda s, *refs: body(s, *refs[k:]),
        grid_spec=pltpu.PrefetchScalarGridSpec(
            num_scalar_prefetch=1,
            grid=(steps,),
            in_specs=[pl.BlockSpec(memory_space=pl.ANY)] * k
            + [full(x.shape) for x in xs]
            + [lanes(a) for a in (*pgs, *arrived)],
            out_specs=[lanes(o) for o in outs],
        ),
        out_shape=outs,
        compiler_params=pltpu.CompilerParams(vmem_limit_bytes=SHARE_VMEM),
        cost_estimate=pl.CostEstimate(
            flops=6 * 1000 * 1000 * 1000, bytes_accessed=24 << 20, transcendentals=0
        ),
    )(scal, *after, *xs, *pgs, *arrived)


def on_device(n, replicas, tokens, expert_ids, gate_probs, cotangent, gate_up, down_weights):
    local, count = gate_up.shape[1], tokens.shape[0]
    low = replicas // HALVES
    z, r = lax.axis_index("expert"), lax.axis_index("replica")
    scal = jnp.stack([z * local, r // low, r % low]).astype(jnp.int32)
    ring = [(i, (i + 1) % n) for i in range(n)]
    across = [(i, (i + low) % replicas) for i in range(replicas)]

    pays = [pack(expert_ids, gate_probs, tokens, cotangent, n * local)]
    others = []
    wgu = jnp.transpose(gate_up, (1, 0, 2))
    for d in range(n):
        others.append(lax.ppermute(pays[d], "replica", across))
        if d < n - 1:
            pays.append(lax.ppermute(pays[d], "expert", ring))
            if d == 0:
                pays[1], others[0], wgu, down_weights = lax.optimization_barrier(
                    (pays[1], others[0], wgu, down_weights)
                )

    wd = jnp.transpose(down_weights, (1, 0, 2))

    def add(got, mine):
        return (got.astype(F32) + mine.astype(F32)).astype(BF)

    step = -(-n // 4)
    stages, sums, totals, before = [], {}, [], ()
    for start in range(0, n, step):
        ready = [d for d in range(start + 1, start + step + 1) if d < n] + ([0] if start == step else [])
        outs, part = stage(scal, EARLY_VMEM if start <= step else STAGE_VMEM, [pays[d] for d in ready], others[start : start + step], count, wgu, wd, before)
        stages.append(outs)
        sums.update(zip(ready, part))
        before = (outs[3],)
        for d in ready:
            if d:
                totals.append(add(lax.ppermute(totals[-1], "expert", ring), sums[d]) if totals else sums[d])
                before = (outs[3], totals[-1])
    steps = [[(i, i // low * low + (i % low + j) % low) for i in range(replicas)] for j in range(1, low)]
    pieces = []
    for start in range(0, local, -(-local // 2)):
        gates, downs, own_down = send_blocks(scal, low, stages, start, -(-local // 2))
        gates = [lax.ppermute(b, "replica", s) for b, s in zip(gates, steps)]
        downs = [lax.ppermute(b, "replica", s) for b, s in zip(downs, steps)]
        pieces.append((*gates, *downs, own_down))
    arrived = lax.ppermute(totals[-1], "expert", ring)
    gate_up_gradient, down_gradient = keep_blocks(scal, low, stages, pieces)
    arrived, gate_up_gradient, down_gradient = lax.optimization_barrier((arrived, gate_up_gradient, down_gradient))
    combined, token_gradient = add(arrived[:count], sums[0][:count]), add(arrived[count : 2 * count], sums[0][count : 2 * count])
    dots = arrived[2 * count :, : 2 * count].astype(F32) + sums[0][2 * count :, : 2 * count].astype(F32)
    dots = dots[:, :count] + dots[:, count:]
    named = expert_ids.T[:, None, :] == jnp.arange(n * local, dtype=jnp.int32)[None, :, None]
    prob_gradient = jnp.sum(jnp.where(named, dots[None], 0.0), axis=1).T
    return (combined, token_gradient, prob_gradient, gate_up_gradient, down_gradient)


def solution(mesh):
    rows = P(("groups", "expert", "replica"), None)
    weights = P(None, "expert", None)
    shares = P(("groups", "replica"), "expert", None)
    return jax.shard_map(
        functools.partial(on_device, mesh.shape["expert"], mesh.shape["replica"]),
        mesh=mesh,
        in_specs=(rows, rows, rows, rows, weights, weights),
        out_specs=(rows, rows, rows, shares, shares),
        check_vma=False,
    )
```

```python
import functools

import jax
import jax.numpy as jnp
from jax import lax
from jax.experimental import pallas as pl
from jax.experimental.pallas import tpu as pltpu
from jax.sharding import PartitionSpec as P

CAP = 64
HALVES = 2
EARLY_VMEM = 34 * 1024 * 1024
STAGE_VMEM = 34 * 1024 * 1024
PACK_VMEM = 60 * 1024 * 1024
SHARE_VMEM = 16 * 1024 * 1024
BF = jnp.bfloat16
F32 = jnp.float32


def mm(a, b):
    return jnp.dot(a, b, preferred_element_type=F32)


def mm_t0(a, b):
    return lax.dot_general(a, b, (((0,), (0,)), ((), ())), preferred_element_type=F32)


def mm_t1(a, b):
    return lax.dot_general(a, b, (((1,), (1,)), ((), ())), preferred_element_type=F32)


def full(shape):
    return pl.BlockSpec(shape, lambda e, s: (0,) * len(shape))


def per_expert(shape):
    return pl.BlockSpec((1,) + tuple(shape[1:]), lambda e, s: (e,) + (0,) * (len(shape) - 1))


def pack_kernel(ids_ref, probs_ref, tok_ref, cot_ref, out_ref):
    top, count = ids_ref.shape
    experts = out_ref.shape[0] - 2 * count
    out_ref[:count, :] = tok_ref[...]
    out_ref[count : 2 * count, :] = cot_ref[...]
    ids, probs = ids_ref[...], probs_ref[...].astype(F32)
    expert = lax.broadcasted_iota(jnp.int32, (experts, count), 0)
    member = jnp.zeros((experts, count), F32)
    weight = jnp.zeros((experts, count), F32)
    for k in range(top):
        hit = ids[k : k + 1, :] == expert
        member = member + hit.astype(F32)
        weight = weight + jnp.where(hit, probs[k : k + 1, :], 0.0)
    row = lax.broadcasted_iota(jnp.int32, (count, count), 0)
    col = lax.broadcasted_iota(jnp.int32, (count, count), 1)
    rank = mm(member.astype(BF), (row < col).astype(F32).astype(BF))
    slot = jnp.where(member > 0.0, rank, -1.0)
    rest = jnp.zeros((experts, out_ref.shape[1] - 2 * count), F32)
    out_ref[2 * count :, :] = jnp.concatenate([slot, weight, rest], axis=1).astype(BF)


def pack(ids, probs, tokens, cot, experts):
    count, width = tokens.shape
    return pl.pallas_call(
        pack_kernel,
        out_shape=jax.ShapeDtypeStruct((2 * count + experts, width), BF),
        compiler_params=pltpu.CompilerParams(vmem_limit_bytes=PACK_VMEM),
    )(ids.T, probs.T, tokens, cot)


def masks(pay, count, first, local):
    experts = pay.shape[0] - 2 * count
    named = lax.broadcasted_iota(jnp.int32, (CAP, experts), 1)
    pick = jnp.concatenate([(named == first + i).astype(F32) for i in range(local)], axis=0).astype(BF)
    slot = lax.broadcasted_iota(jnp.int32, (CAP, count), 0).astype(F32)
    slot = jnp.concatenate([slot] * local, axis=0)
    hit = mm(pick, pay[2 * count :, :count]) == slot
    weight = jnp.where(hit, mm(pick, pay[2 * count :, count : 2 * count]), 0.0)
    return hit.astype(F32), weight


def scatter_slots(dst, values, d, local):
    for i in range(local):
        dst[i, d * CAP : (d + 1) * CAP, :] = values[i * CAP : (i + 1) * CAP, :]


def act_gradient(pre, hidden_grad):
    middle = pre.shape[-1] // 2
    g, u = pre[:, :middle], pre[:, middle:]
    s = jax.nn.sigmoid(g)
    return jnp.concatenate(
        [hidden_grad * u * s * (1.0 + g * (1.0 - s)), hidden_grad * g * s], axis=-1
    ).astype(BF)


def stage_kernel(m, own, local, count, after, scal, *refs):
    pays, (wgu, wd) = refs[:m], refs[m : m + 2]
    refs = refs[m + 2 + after :]
    x_ref, h_ref, pg_ref, gs_ref = refs[:4]
    sums, refs = refs[4 : 4 + own], refs[4 + own :]
    xs, hs = refs[:2]
    if own:
        hit_s, wt_s, cs, o_s, dx_s, dots_s = refs[2:]
    e = pl.program_id(0)
    here = pl.ds(pl.multiple_of(e * CAP, CAP), CAP)

    @pl.when(e == 0)
    def _():
        for d in range(m):
            hit, weight = masks(pays[d], count, scal[0], local)
            hit_b = hit.astype(BF)
            scatter_slots(xs, mm(hit_b, pays[d][:count, :]).astype(BF), d, local)
            if d < own:
                hit_s[d] = hit_b
                wt_s[d] = weight.astype(BF)
                slots = mm(hit_b, pays[d][count : 2 * count, :])
                scatter_slots(cs, slots.astype(BF), d, local)
                slots = jnp.sum(weight, axis=1, keepdims=True) * slots
            else:
                slots = mm(weight.astype(BF), pays[d][count : 2 * count, :])
            scatter_slots(gs_ref, slots.astype(BF), d, local)

    half_d, half_f = x_ref.shape[-1], h_ref.shape[-1]
    x_ref[0] = xs[e, :, pl.ds(pl.multiple_of(scal[1] * half_d, half_d), half_d)]
    pre = mm(xs[e], wgu[0])
    middle = pre.shape[-1] // 2
    hidden = (jax.nn.silu(pre[:, :middle]) * pre[:, middle:]).astype(BF)
    hs[...] = hidden
    h_ref[0] = hs[:, pl.ds(pl.multiple_of(scal[1] * half_f, half_f), half_f)]
    pg = act_gradient(pre, mm_t1(gs_ref[e], wd[0]))
    pg_ref[0] = pg
    if own:
        out = mm(hidden[: own * CAP], wd[0]).astype(BF)
        dots = jnp.sum(cs[e].astype(F32) * out.astype(F32), axis=1, keepdims=True)
        dx = mm_t1(pg[: own * CAP], wgu[0]).astype(BF)
        for d in range(own):
            part = slice(d * CAP, (d + 1) * CAP)
            o_s[d, here, :] = out[part]
            dx_s[d, here, :] = dx[part]
            spread = hit_s[d, here, :].astype(F32) * dots[part]
            dots_s[d, pl.ds(e, 1), :] = jnp.sum(spread, axis=0, keepdims=True)

        @pl.when(e == local - 1)
        def _():
            for d in range(own):
                sums[d][:count, :] = mm_t0(wt_s[d], o_s[d]).astype(BF)
                sums[d][count : 2 * count, :] = mm_t0(hit_s[d], dx_s[d]).astype(BF)
                experts, width = sums[d].shape[0] - 2 * count, sums[d].shape[1]
                row = lax.broadcasted_iota(jnp.int32, (experts, count), 0)
                dots = jnp.zeros((experts, count), F32)
                for i in range(local):
                    dots = dots + jnp.where(row == scal[0] + i, dots_s[d, i : i + 1, :], 0.0)
                upper = dots.astype(BF).astype(F32)
                rest = jnp.zeros((experts, width - 2 * count), F32)
                sums[d][2 * count :, :] = jnp.concatenate([upper, dots - upper, rest], axis=1).astype(BF)


def stage(scal, limit, mine, others, count, wgu, wd, after=()):
    pays = (*mine, *others)
    m, own, (local, width, two_f) = len(pays), len(mine), wgu.shape
    rows, ff = m * CAP, two_f // 2
    outs = [
        (jax.ShapeDtypeStruct((local, rows, width // HALVES), BF), per_expert((local, rows, width // HALVES))),
        (jax.ShapeDtypeStruct((local, rows, ff // HALVES), BF), per_expert((local, rows, ff // HALVES))),
        (jax.ShapeDtypeStruct((local, rows, two_f), BF), per_expert((local, rows, two_f))),
        (jax.ShapeDtypeStruct((local, rows, width), BF), full((local, rows, width))),
    ]
    outs += [(jax.ShapeDtypeStruct(a.shape, BF), full(a.shape)) for a in mine]
    scratch = [pltpu.VMEM((local, rows, width), BF), pltpu.VMEM((rows, ff), BF)]
    if own:
        scratch += [
            pltpu.VMEM((own, local * CAP, count), BF),
            pltpu.VMEM((own, local * CAP, count), BF),
            pltpu.VMEM((local, own * CAP, width), BF),
            pltpu.VMEM((own, local * CAP, width), BF),
            pltpu.VMEM((own, local * CAP, width), BF),
            pltpu.VMEM((own, local, count), F32),
        ]
    res = pl.pallas_call(
        functools.partial(stage_kernel, m, own, local, count, len(after)),
        grid_spec=pltpu.PrefetchScalarGridSpec(
            num_scalar_prefetch=1,
            grid=(local,),
            in_specs=[full(a.shape) for a in pays]
            + [per_expert(wgu.shape), per_expert(wd.shape)]
            + [pl.BlockSpec(memory_space=pl.ANY)] * len(after),
            out_specs=[o[1] for o in outs],
            scratch_shapes=scratch,
        ),
        out_shape=[o[0] for o in outs],
        compiler_params=pltpu.CompilerParams(vmem_limit_bytes=limit),
        cost_estimate=pl.CostEstimate(
            flops=(14 if own else 7) * 1000 * 1000 * 1000, bytes_accessed=24 << 20, transcendentals=local * rows * ff
        ),
    )(scal, *pays, wgu, wd, *after)
    return res[:4], list(res[4:])


def send_kernel(parts, low, scal, *refs):
    xs, hs, pgs, gss = (refs[k * parts : (k + 1) * parts] for k in range(4))
    gates, downs, own_down, acc_d = refs[4 * parts : 4 * parts + low - 1], refs[4 * parts + low - 1 : -2], refs[-2], refs[-1]
    lo = scal[2]
    pg = jnp.concatenate([p[0] for p in pgs], axis=0)
    size = xs[0].shape[-1] // low
    for j in range(1, low):
        cols = pl.ds(pl.multiple_of(lax.rem(lo + j, low) * size, size), size)
        gates[j - 1][0] = mm_t0(jnp.concatenate([x[0, :, cols] for x in xs], axis=0), pg).astype(BF)
    h = jnp.concatenate([h_[0] for h_ in hs], axis=0)
    acc_d[...] = mm_t0(h, jnp.concatenate([g[0] for g in gss], axis=0))
    size = acc_d.shape[0] // low
    for j in range(low):
        block = acc_d[pl.ds(pl.multiple_of(lax.rem(lo + j, low) * size, size), size), :]
        if j:
            downs[j - 1][0] = block.astype(BF)
        else:
            own_down[0] = block


def send_blocks(scal, low, stages, start, local, after=()):
    xs, hs, pgs, gss = zip(*stages)
    width, ff = gss[0].shape[-1], pgs[0].shape[-1] // 2
    half_d, half_f = xs[0].shape[-1], hs[0].shape[-1]
    whole = lambda a: pl.BlockSpec((1,) + a.shape[1:], lambda e, s: (e + start, 0, 0))
    gate_shape, down_shape = (local, half_d // low, 2 * ff), (local, half_f // low, width)
    outs = [jax.ShapeDtypeStruct(gate_shape, BF)] * (low - 1)
    outs += [jax.ShapeDtypeStruct(down_shape, BF)] * (low - 1) + [jax.ShapeDtypeStruct(down_shape, F32)]
    k = len(after)
    body = functools.partial(send_kernel, len(stages), low)
    res = pl.pallas_call(
        lambda s, *refs: body(s, *refs[k:]),
        grid_spec=pltpu.PrefetchScalarGridSpec(
            num_scalar_prefetch=1,
            grid=(local,),
            in_specs=[pl.BlockSpec(memory_space=pl.ANY)] * k
            + [whole(a) for a in (*xs, *hs, *pgs, *gss)],
            out_specs=[per_expert(o.shape) for o in outs],
            scratch_shapes=[pltpu.VMEM((half_f, width), F32)],
        ),
        out_shape=outs,
        compiler_params=pltpu.CompilerParams(vmem_limit_bytes=SHARE_VMEM),
        cost_estimate=pl.CostEstimate(
            flops=0, bytes_accessed=1 << 10, transcendentals=0
        ),
    )(scal, *after, *xs, *hs, *pgs, *gss)
    return res[: low - 1], res[low - 1 : 2 * low - 2], res[-1]


def own_kernel(parts, low, scal, *refs):
    xs, pgs, out_ref = refs[:parts], refs[parts : 2 * parts], refs[-1]
    size = xs[0].shape[-1] // low
    cols = pl.ds(pl.multiple_of(scal[2] * size, size), size)
    out_ref[0] = mm_t0(
        jnp.concatenate([x[0, :, cols] for x in xs], axis=0), jnp.concatenate([p[0] for p in pgs], axis=0)
    )


def own_blocks(scal, low, stages, after):
    xs, _, pgs, _ = zip(*stages)
    out = jax.ShapeDtypeStruct((xs[0].shape[0], xs[0].shape[-1] // low, pgs[0].shape[-1]), F32)
    return pl.pallas_call(
        functools.partial(own_kernel, len(stages), low),
        grid_spec=pltpu.PrefetchScalarGridSpec(
            num_scalar_prefetch=1,
            grid=(out.shape[0],),
            in_specs=[per_expert(a.shape) for a in (*xs, *pgs)] + [pl.BlockSpec(memory_space=pl.ANY)] * len(after),
            out_specs=per_expert(out.shape),
        ),
        out_shape=out,
        compiler_params=pltpu.CompilerParams(vmem_limit_bytes=SHARE_VMEM),
        cost_estimate=pl.CostEstimate(flops=0, bytes_accessed=1 << 10, transcendentals=0),
    )(scal, *xs, *pgs, *after)


def join_kernel(pieces, low, own_ref, *refs):
    gate_ref, down_ref = refs[-2:]
    e = 0
    for k in range(pieces):
        arrived = refs[k * (2 * low - 1) : (k + 1) * (2 * low - 1)]
        for i in range(arrived[-1].shape[0]):
            gate_ref[:, e, :] = own_ref[e] + sum(g[i].astype(F32) for g in arrived[: low - 1])
            down_ref[:, e, :] = arrived[-1][i] + sum(g[i].astype(F32) for g in arrived[low - 1 : -1])
            e += 1


def join_blocks(low, own, pieces):
    arrived = [a for piece in pieces for a in piece]
    local, steps = own.shape[0], 4
    lanes = lambda a: pl.BlockSpec(a.shape[:-1] + (a.shape[-1] // steps,), lambda c: (0, 0, c))
    outs = [
        jax.ShapeDtypeStruct((a.shape[1], local, a.shape[-1]), F32) for a in (own, pieces[0][-1])
    ]
    return pl.pallas_call(
        functools.partial(join_kernel, len(pieces), low),
        grid=(steps,),
        in_specs=[lanes(a) for a in (own, *arrived)],
        out_specs=[lanes(o) for o in outs],
        out_shape=outs,
        compiler_params=pltpu.CompilerParams(vmem_limit_bytes=SHARE_VMEM),
        cost_estimate=pl.CostEstimate(flops=5 * 1000 * 1000 * 1000, bytes_accessed=16 << 20, transcendentals=0),
    )(own, *arrived)


def on_device(n, replicas, tokens, expert_ids, gate_probs, cotangent, gate_up, down_weights):
    local, count = gate_up.shape[1], tokens.shape[0]
    low = replicas // HALVES
    z, r = lax.axis_index("expert"), lax.axis_index("replica")
    scal = jnp.stack([z * local, r // low, r % low]).astype(jnp.int32)
    ring = [(i, (i + 1) % n) for i in range(n)]
    across = [(i, (i + low) % replicas) for i in range(replicas)]

    pays = [pack(expert_ids, gate_probs, tokens, cotangent, n * local)]
    others = []
    wgu = jnp.transpose(gate_up, (1, 0, 2))
    for d in range(n):
        others.append(lax.ppermute(pays[d], "replica", across))
        if d < n - 1:
            pays.append(lax.ppermute(pays[d], "expert", ring))
            if d == 0:
                pays[1], others[0], wgu, down_weights = lax.optimization_barrier(
                    (pays[1], others[0], wgu, down_weights)
                )

    wd = jnp.transpose(down_weights, (1, 0, 2))

    def add(got, mine):
        return (got.astype(F32) + mine.astype(F32)).astype(BF)

    step = -(-n // 4)
    stages, sums, totals, before = [], {}, [], ()
    for start in range(0, n, step):
        ready = [d for d in range(start + 1, start + step + 1) if d < n] + ([0] if start == step else [])
        outs, part = stage(scal, EARLY_VMEM if start <= step else STAGE_VMEM, [pays[d] for d in ready], others[start : start + step], count, wgu, wd, before)
        stages.append(outs)
        sums.update(zip(ready, part))
        before = (outs[3],)
        for d in ready:
            if d:
                if totals:
                    send, _ = lax.optimization_barrier((totals[-1], pays[d]))
                    totals.append(add(lax.ppermute(send, "expert", ring), sums[d]))
                else:
                    totals.append(sums[d])
                before = (outs[3], totals[-1])
    steps = [[(i, i // low * low + (i % low + j) % low) for i in range(replicas)] for j in range(1, low)]
    arrived = lax.ppermute(totals[-1], "expert", ring)
    last = local // 2
    pieces, sent = [], ()
    for start, size in ((0, last), (last, local - last)) if last else ((0, local),):
        gates, downs, own_down = send_blocks(scal, low, stages, start, size)
        sent = (*gates, *downs)
        if start:
            gates, downs, arrived = lax.optimization_barrier((gates, downs, arrived))
        gates = [lax.ppermute(b, "replica", s) for b, s in zip(gates, steps)]
        downs = [lax.ppermute(b, "replica", s) for b, s in zip(downs, steps)]
        pieces.append((*gates, *downs, own_down))
    own = own_blocks(scal, low, stages, sent)
    gate_up_gradient, down_gradient = join_blocks(low, own, pieces)
    combined, token_gradient = add(arrived[:count], sums[0][:count]), add(arrived[count : 2 * count], sums[0][count : 2 * count])
    dots = arrived[2 * count :, : 2 * count].astype(F32) + sums[0][2 * count :, : 2 * count].astype(F32)
    dots = dots[:, :count] + dots[:, count:]
    named = expert_ids.T[:, None, :] == jnp.arange(n * local, dtype=jnp.int32)[None, :, None]
    prob_gradient = jnp.sum(jnp.where(named, dots[None], 0.0), axis=1).T
    return (combined, token_gradient, prob_gradient, gate_up_gradient, down_gradient)


def solution(mesh):
    rows = P(("groups", "expert", "replica"), None)
    weights = P(None, "expert", None)
    shares = P(("groups", "replica"), "expert", None)
    return jax.shard_map(
        functools.partial(on_device, mesh.shape["expert"], mesh.shape["replica"]),
        mesh=mesh,
        in_specs=(rows, rows, rows, rows, weights, weights),
        out_specs=(rows, rows, rows, shares, shares),
        check_vma=False,
    )
```

```python
import functools

import jax
import jax.numpy as jnp
from jax import lax
from jax.experimental import pallas as pl
from jax.experimental.pallas import tpu as pltpu
from jax.sharding import PartitionSpec as P

CAP = 64
HALVES = 2
EARLY_VMEM = 34 * 1024 * 1024
STAGE_VMEM = 34 * 1024 * 1024
PACK_VMEM = 60 * 1024 * 1024
SHARE_VMEM = 16 * 1024 * 1024
BF = jnp.bfloat16
F32 = jnp.float32


def mm(a, b):
    return jnp.dot(a, b, preferred_element_type=F32)


def mm_t0(a, b):
    return lax.dot_general(a, b, (((0,), (0,)), ((), ())), preferred_element_type=F32)


def mm_t1(a, b):
    return lax.dot_general(a, b, (((1,), (1,)), ((), ())), preferred_element_type=F32)


def full(shape):
    return pl.BlockSpec(shape, lambda e, s: (0,) * len(shape))


def per_expert(shape):
    return pl.BlockSpec((1,) + tuple(shape[1:]), lambda e, s: (e,) + (0,) * (len(shape) - 1))


def pack_kernel(ids_ref, probs_ref, tok_ref, cot_ref, out_ref):
    top, count = ids_ref.shape
    experts = out_ref.shape[0] - 2 * count
    out_ref[:count, :] = tok_ref[...]
    out_ref[count : 2 * count, :] = cot_ref[...]
    ids, probs = ids_ref[...], probs_ref[...].astype(F32)
    expert = lax.broadcasted_iota(jnp.int32, (experts, count), 0)
    member = jnp.zeros((experts, count), F32)
    weight = jnp.zeros((experts, count), F32)
    for k in range(top):
        hit = ids[k : k + 1, :] == expert
        member = member + hit.astype(F32)
        weight = weight + jnp.where(hit, probs[k : k + 1, :], 0.0)
    row = lax.broadcasted_iota(jnp.int32, (count, count), 0)
    col = lax.broadcasted_iota(jnp.int32, (count, count), 1)
    rank = mm(member.astype(BF), (row < col).astype(F32).astype(BF))
    slot = jnp.where(member > 0.0, rank, -1.0)
    rest = jnp.zeros((experts, out_ref.shape[1] - 2 * count), F32)
    out_ref[2 * count :, :] = jnp.concatenate([slot, weight, rest], axis=1).astype(BF)


def pack(ids, probs, tokens, cot, experts):
    count, width = tokens.shape
    return pl.pallas_call(
        pack_kernel,
        out_shape=jax.ShapeDtypeStruct((2 * count + experts, width), BF),
        compiler_params=pltpu.CompilerParams(vmem_limit_bytes=PACK_VMEM),
    )(ids.T, probs.T, tokens, cot)


def masks(pay, count, first, local):
    experts = pay.shape[0] - 2 * count
    named = lax.broadcasted_iota(jnp.int32, (CAP, experts), 1)
    pick = jnp.concatenate([(named == first + i).astype(F32) for i in range(local)], axis=0).astype(BF)
    slot = lax.broadcasted_iota(jnp.int32, (CAP, count), 0).astype(F32)
    slot = jnp.concatenate([slot] * local, axis=0)
    hit = mm(pick, pay[2 * count :, :count]) == slot
    weight = jnp.where(hit, mm(pick, pay[2 * count :, count : 2 * count]), 0.0)
    return hit.astype(F32), weight


def scatter_slots(dst, values, d, local):
    for i in range(local):
        dst[i, d * CAP : (d + 1) * CAP, :] = values[i * CAP : (i + 1) * CAP, :]


def act_gradient(pre, hidden_grad):
    middle = pre.shape[-1] // 2
    g, u = pre[:, :middle], pre[:, middle:]
    s = jax.nn.sigmoid(g)
    return jnp.concatenate(
        [hidden_grad * u * s * (1.0 + g * (1.0 - s)), hidden_grad * g * s], axis=-1
    ).astype(BF)


def stage_kernel(m, own, local, count, after, scal, *refs):
    pays, (wgu, wd) = refs[:m], refs[m : m + 2]
    refs = refs[m + 2 + after :]
    x_ref, h_ref, pg_ref, gs_ref = refs[:4]
    sums, refs = refs[4 : 4 + own], refs[4 + own :]
    xs, hs, gu_s, d_s, sem = refs[:5]
    if own:
        hit_s, wt_s, cs, o_s, dx_s, dots_s = refs[5:]
    e = pl.program_id(0)
    here = pl.ds(pl.multiple_of(e * CAP, CAP), CAP)

    def fetch(k):
        slot = lax.rem(k, 2)
        return (
            pltpu.make_async_copy(wgu.at[k], gu_s.at[slot], sem.at[0, slot]),
            pltpu.make_async_copy(wd.at[k], d_s.at[slot], sem.at[1, slot]),
        )

    @pl.when(e == 0)
    def _():
        for copy in fetch(e):
            copy.start()

    @pl.when(e + 1 < local)
    def _():
        for copy in fetch(e + 1):
            copy.start()

    @pl.when(e == 0)
    def _():
        for d in range(m):
            hit, weight = masks(pays[d], count, scal[0], local)
            hit_b = hit.astype(BF)
            scatter_slots(xs, mm(hit_b, pays[d][:count, :]).astype(BF), d, local)
            if d < own:
                hit_s[d] = hit_b
                wt_s[d] = weight.astype(BF)
                slots = mm(hit_b, pays[d][count : 2 * count, :])
                scatter_slots(cs, slots.astype(BF), d, local)
                slots = jnp.sum(weight, axis=1, keepdims=True) * slots
            else:
                slots = mm(weight.astype(BF), pays[d][count : 2 * count, :])
            scatter_slots(gs_ref, slots.astype(BF), d, local)

    half_d, half_f = x_ref.shape[-1], h_ref.shape[-1]
    x_ref[0] = xs[e, :, pl.ds(pl.multiple_of(scal[1] * half_d, half_d), half_d)]
    for copy in fetch(e):
        copy.wait()
    slot = lax.rem(e, 2)
    pre = mm(xs[e], gu_s[slot])
    middle = pre.shape[-1] // 2
    hidden = (jax.nn.silu(pre[:, :middle]) * pre[:, middle:]).astype(BF)
    hs[...] = hidden
    h_ref[0] = hs[:, pl.ds(pl.multiple_of(scal[1] * half_f, half_f), half_f)]
    pg = act_gradient(pre, mm_t1(gs_ref[e], d_s[slot]))
    pg_ref[0] = pg
    if own:
        out = mm(hidden[: own * CAP], d_s[slot]).astype(BF)
        dots = jnp.sum(cs[e].astype(F32) * out.astype(F32), axis=1, keepdims=True)
        dx = mm_t1(pg[: own * CAP], gu_s[slot]).astype(BF)
        for d in range(own):
            part = slice(d * CAP, (d + 1) * CAP)
            o_s[d, here, :] = out[part]
            dx_s[d, here, :] = dx[part]
            spread = hit_s[d, here, :].astype(F32) * dots[part]
            dots_s[d, pl.ds(e, 1), :] = jnp.sum(spread, axis=0, keepdims=True)

        @pl.when(e == local - 1)
        def _():
            for d in range(own):
                sums[d][:count, :] = mm_t0(wt_s[d], o_s[d]).astype(BF)
                sums[d][count : 2 * count, :] = mm_t0(hit_s[d], dx_s[d]).astype(BF)
                experts, width = sums[d].shape[0] - 2 * count, sums[d].shape[1]
                row = lax.broadcasted_iota(jnp.int32, (experts, count), 0)
                dots = jnp.zeros((experts, count), F32)
                for i in range(local):
                    dots = dots + jnp.where(row == scal[0] + i, dots_s[d, i : i + 1, :], 0.0)
                upper = dots.astype(BF).astype(F32)
                rest = jnp.zeros((experts, width - 2 * count), F32)
                sums[d][2 * count :, :] = jnp.concatenate([upper, dots - upper, rest], axis=1).astype(BF)


def stage(scal, limit, mine, others, count, wgu, wd, after=()):
    pays = (*mine, *others)
    m, own, (local, width, two_f) = len(pays), len(mine), wgu.shape
    rows, ff = m * CAP, two_f // 2
    outs = [
        (jax.ShapeDtypeStruct((local, rows, width // HALVES), BF), per_expert((local, rows, width // HALVES))),
        (jax.ShapeDtypeStruct((local, rows, ff // HALVES), BF), per_expert((local, rows, ff // HALVES))),
        (jax.ShapeDtypeStruct((local, rows, two_f), BF), per_expert((local, rows, two_f))),
        (jax.ShapeDtypeStruct((local, rows, width), BF), full((local, rows, width))),
    ]
    outs += [(jax.ShapeDtypeStruct(a.shape, BF), full(a.shape)) for a in mine]
    scratch = [
        pltpu.VMEM((local, rows, width), BF),
        pltpu.VMEM((rows, ff), BF),
        pltpu.VMEM((2,) + wgu.shape[1:], BF),
        pltpu.VMEM((2,) + wd.shape[1:], BF),
        pltpu.SemaphoreType.DMA((2, 2)),
    ]
    if own:
        scratch += [
            pltpu.VMEM((own, local * CAP, count), BF),
            pltpu.VMEM((own, local * CAP, count), BF),
            pltpu.VMEM((local, own * CAP, width), BF),
            pltpu.VMEM((own, local * CAP, width), BF),
            pltpu.VMEM((own, local * CAP, width), BF),
            pltpu.VMEM((own, local, count), F32),
        ]
    res = pl.pallas_call(
        functools.partial(stage_kernel, m, own, local, count, len(after)),
        grid_spec=pltpu.PrefetchScalarGridSpec(
            num_scalar_prefetch=1,
            grid=(local,),
            in_specs=[full(a.shape) for a in pays]
            + [pl.BlockSpec(memory_space=pl.ANY)] * (2 + len(after)),
            out_specs=[o[1] for o in outs],
            scratch_shapes=scratch,
        ),
        out_shape=[o[0] for o in outs],
        compiler_params=pltpu.CompilerParams(vmem_limit_bytes=limit),
        cost_estimate=pl.CostEstimate(
            flops=(14 if own else 7) * 1000 * 1000 * 1000, bytes_accessed=24 << 20, transcendentals=local * rows * ff
        ),
    )(scal, *pays, wgu, wd, *after)
    return res[:4], list(res[4:])


def send_kernel(parts, low, scal, *refs):
    xs, hs, pgs, gss = (refs[k * parts : (k + 1) * parts] for k in range(4))
    gates, downs, own_down, acc_d = refs[4 * parts : 4 * parts + low - 1], refs[4 * parts + low - 1 : -2], refs[-2], refs[-1]
    lo = scal[2]
    pg = jnp.concatenate([p[0] for p in pgs], axis=0)
    size = xs[0].shape[-1] // low
    for j in range(1, low):
        cols = pl.ds(pl.multiple_of(lax.rem(lo + j, low) * size, size), size)
        gates[j - 1][0] = mm_t0(jnp.concatenate([x[0, :, cols] for x in xs], axis=0), pg).astype(BF)
    h = jnp.concatenate([h_[0] for h_ in hs], axis=0)
    acc_d[...] = mm_t0(h, jnp.concatenate([g[0] for g in gss], axis=0))
    size = acc_d.shape[0] // low
    for j in range(low):
        block = acc_d[pl.ds(pl.multiple_of(lax.rem(lo + j, low) * size, size), size), :]
        if j:
            downs[j - 1][0] = block.astype(BF)
        else:
            own_down[0] = block


def send_blocks(scal, low, stages, start, local, after=()):
    xs, hs, pgs, gss = zip(*stages)
    width, ff = gss[0].shape[-1], pgs[0].shape[-1] // 2
    half_d, half_f = xs[0].shape[-1], hs[0].shape[-1]
    whole = lambda a: pl.BlockSpec((1,) + a.shape[1:], lambda e, s: (e + start, 0, 0))
    gate_shape, down_shape = (local, half_d // low, 2 * ff), (local, half_f // low, width)
    outs = [jax.ShapeDtypeStruct(gate_shape, BF)] * (low - 1)
    outs += [jax.ShapeDtypeStruct(down_shape, BF)] * (low - 1) + [jax.ShapeDtypeStruct(down_shape, F32)]
    k = len(after)
    body = functools.partial(send_kernel, len(stages), low)
    res = pl.pallas_call(
        lambda s, *refs: body(s, *refs[k:]),
        grid_spec=pltpu.PrefetchScalarGridSpec(
            num_scalar_prefetch=1,
            grid=(local,),
            in_specs=[pl.BlockSpec(memory_space=pl.ANY)] * k
            + [whole(a) for a in (*xs, *hs, *pgs, *gss)],
            out_specs=[per_expert(o.shape) for o in outs],
            scratch_shapes=[pltpu.VMEM((half_f, width), F32)],
        ),
        out_shape=outs,
        compiler_params=pltpu.CompilerParams(vmem_limit_bytes=SHARE_VMEM),
        cost_estimate=pl.CostEstimate(
            flops=0, bytes_accessed=1 << 10, transcendentals=0
        ),
    )(scal, *after, *xs, *hs, *pgs, *gss)
    return res[: low - 1], res[low - 1 : 2 * low - 2], res[-1]


def own_kernel(parts, low, scal, *refs):
    xs, pgs, out_ref = refs[:parts], refs[parts : 2 * parts], refs[-1]
    size = xs[0].shape[-1] // low
    cols = pl.ds(pl.multiple_of(scal[2] * size, size), size)
    out_ref[0] = mm_t0(
        jnp.concatenate([x[0, :, cols] for x in xs], axis=0), jnp.concatenate([p[0] for p in pgs], axis=0)
    )


def own_blocks(scal, low, stages, after):
    xs, _, pgs, _ = zip(*stages)
    out = jax.ShapeDtypeStruct((xs[0].shape[0], xs[0].shape[-1] // low, pgs[0].shape[-1]), F32)
    return pl.pallas_call(
        functools.partial(own_kernel, len(stages), low),
        grid_spec=pltpu.PrefetchScalarGridSpec(
            num_scalar_prefetch=1,
            grid=(out.shape[0],),
            in_specs=[per_expert(a.shape) for a in (*xs, *pgs)] + [pl.BlockSpec(memory_space=pl.ANY)] * len(after),
            out_specs=per_expert(out.shape),
        ),
        out_shape=out,
        compiler_params=pltpu.CompilerParams(vmem_limit_bytes=SHARE_VMEM),
        cost_estimate=pl.CostEstimate(flops=0, bytes_accessed=1 << 10, transcendentals=0),
    )(scal, *xs, *pgs, *after)


def join_kernel(pieces, low, own_ref, *refs):
    gate_ref, down_ref = refs[-2:]
    e = 0
    for k in range(pieces):
        arrived = refs[k * (2 * low - 1) : (k + 1) * (2 * low - 1)]
        for i in range(arrived[-1].shape[0]):
            gate_ref[:, e, :] = own_ref[e] + sum(g[i].astype(F32) for g in arrived[: low - 1])
            down_ref[:, e, :] = arrived[-1][i] + sum(g[i].astype(F32) for g in arrived[low - 1 : -1])
            e += 1


def join_blocks(low, own, pieces):
    arrived = [a for piece in pieces for a in piece]
    local, steps = own.shape[0], 4
    lanes = lambda a: pl.BlockSpec(a.shape[:-1] + (a.shape[-1] // steps,), lambda c: (0, 0, c))
    outs = [
        jax.ShapeDtypeStruct((a.shape[1], local, a.shape[-1]), F32) for a in (own, pieces[0][-1])
    ]
    return pl.pallas_call(
        functools.partial(join_kernel, len(pieces), low),
        grid=(steps,),
        in_specs=[lanes(a) for a in (own, *arrived)],
        out_specs=[lanes(o) for o in outs],
        out_shape=outs,
        compiler_params=pltpu.CompilerParams(vmem_limit_bytes=SHARE_VMEM),
        cost_estimate=pl.CostEstimate(flops=5 * 1000 * 1000 * 1000, bytes_accessed=16 << 20, transcendentals=0),
    )(own, *arrived)


def on_device(n, replicas, tokens, expert_ids, gate_probs, cotangent, gate_up, down_weights):
    local, count = gate_up.shape[1], tokens.shape[0]
    low = replicas // HALVES
    z, r = lax.axis_index("expert"), lax.axis_index("replica")
    scal = jnp.stack([z * local, r // low, r % low]).astype(jnp.int32)
    ring = [(i, (i + 1) % n) for i in range(n)]
    across = [(i, (i + low) % replicas) for i in range(replicas)]

    pays = [pack(expert_ids, gate_probs, tokens, cotangent, n * local)]
    others = []
    wgu = jnp.transpose(gate_up, (1, 0, 2))
    for d in range(n):
        others.append(lax.ppermute(pays[d], "replica", across))
        if d < n - 1:
            pays.append(lax.ppermute(pays[d], "expert", ring))
            if d == 0:
                pays[1], others[0], wgu, down_weights = lax.optimization_barrier(
                    (pays[1], others[0], wgu, down_weights)
                )

    wd = jnp.transpose(down_weights, (1, 0, 2))

    def add(got, mine):
        return (got.astype(F32) + mine.astype(F32)).astype(BF)

    step = -(-n // 4)
    stages, sums, totals, before = [], {}, [], ()
    for start in range(0, n, step):
        ready = [d for d in range(start + 1, start + step + 1) if d < n] + ([0] if start == step else [])
        outs, part = stage(scal, EARLY_VMEM if start <= step else STAGE_VMEM, [pays[d] for d in ready], others[start : start + step], count, wgu, wd, before)
        stages.append(outs)
        sums.update(zip(ready, part))
        before = (outs[3],)
        for d in ready:
            if d:
                if totals:
                    send, _ = lax.optimization_barrier((totals[-1], pays[d]))
                    totals.append(add(lax.ppermute(send, "expert", ring), sums[d]))
                else:
                    totals.append(sums[d])
                before = (outs[3], totals[-1])
    steps = [[(i, i // low * low + (i % low + j) % low) for i in range(replicas)] for j in range(1, low)]
    arrived = lax.ppermute(totals[-1], "expert", ring)
    last = local // 2
    pieces, sent = [], ()
    for start, size in ((0, last), (last, local - last)) if last else ((0, local),):
        gates, downs, own_down = send_blocks(scal, low, stages, start, size)
        sent = (*gates, *downs)
        if start:
            gates, downs, arrived = lax.optimization_barrier((gates, downs, arrived))
        gates = [lax.ppermute(b, "replica", s) for b, s in zip(gates, steps)]
        downs = [lax.ppermute(b, "replica", s) for b, s in zip(downs, steps)]
        pieces.append((*gates, *downs, own_down))
    own = own_blocks(scal, low, stages, sent)
    gate_up_gradient, down_gradient = join_blocks(low, own, pieces)
    combined, token_gradient = add(arrived[:count], sums[0][:count]), add(arrived[count : 2 * count], sums[0][count : 2 * count])
    dots = arrived[2 * count :, : 2 * count].astype(F32) + sums[0][2 * count :, : 2 * count].astype(F32)
    dots = dots[:, :count] + dots[:, count:]
    named = expert_ids.T[:, None, :] == jnp.arange(n * local, dtype=jnp.int32)[None, :, None]
    prob_gradient = jnp.sum(jnp.where(named, dots[None], 0.0), axis=1).T
    return (combined, token_gradient, prob_gradient, gate_up_gradient, down_gradient)


def solution(mesh):
    rows = P(("groups", "expert", "replica"), None)
    weights = P(None, "expert", None)
    shares = P(("groups", "replica"), "expert", None)
    return jax.shard_map(
        functools.partial(on_device, mesh.shape["expert"], mesh.shape["replica"]),
        mesh=mesh,
        in_specs=(rows, rows, rows, rows, weights, weights),
        out_specs=(rows, rows, rows, shares, shares),
        check_vma=False,
    )
```

```python
import functools

import jax
import jax.numpy as jnp
from jax import lax
from jax.experimental import pallas as pl
from jax.experimental.pallas import tpu as pltpu
from jax.sharding import PartitionSpec as P

CAP = 64
HALVES = 2
EARLY_VMEM = 34 * 1024 * 1024
STAGE_VMEM = 34 * 1024 * 1024
PACK_VMEM = 60 * 1024 * 1024
SHARE_VMEM = 24 * 1024 * 1024
BF = jnp.bfloat16
F32 = jnp.float32


def mm(a, b):
    return jnp.dot(a, b, preferred_element_type=F32)


def mm_t0(a, b):
    return lax.dot_general(a, b, (((0,), (0,)), ((), ())), preferred_element_type=F32)


def mm_t1(a, b):
    return lax.dot_general(a, b, (((1,), (1,)), ((), ())), preferred_element_type=F32)


def full(shape):
    return pl.BlockSpec(shape, lambda e, s: (0,) * len(shape))


def per_expert(shape):
    return pl.BlockSpec((1,) + tuple(shape[1:]), lambda e, s: (e,) + (0,) * (len(shape) - 1))


def pack_kernel(ids_ref, probs_ref, tok_ref, cot_ref, out_ref):
    top, count = ids_ref.shape
    experts = out_ref.shape[0] - 2 * count
    out_ref[:count, :] = tok_ref[...]
    out_ref[count : 2 * count, :] = cot_ref[...]
    ids, probs = ids_ref[...], probs_ref[...].astype(F32)
    expert = lax.broadcasted_iota(jnp.int32, (experts, count), 0)
    member = jnp.zeros((experts, count), F32)
    weight = jnp.zeros((experts, count), F32)
    for k in range(top):
        hit = ids[k : k + 1, :] == expert
        member = member + hit.astype(F32)
        weight = weight + jnp.where(hit, probs[k : k + 1, :], 0.0)
    row = lax.broadcasted_iota(jnp.int32, (count, count), 0)
    col = lax.broadcasted_iota(jnp.int32, (count, count), 1)
    rank = mm(member.astype(BF), (row < col).astype(F32).astype(BF))
    slot = jnp.where(member > 0.0, rank, -1.0)
    rest = jnp.zeros((experts, out_ref.shape[1] - 2 * count), F32)
    out_ref[2 * count :, :] = jnp.concatenate([slot, weight, rest], axis=1).astype(BF)


def pack(ids, probs, tokens, cot, experts):
    count, width = tokens.shape
    return pl.pallas_call(
        pack_kernel,
        out_shape=jax.ShapeDtypeStruct((2 * count + experts, width), BF),
        compiler_params=pltpu.CompilerParams(vmem_limit_bytes=PACK_VMEM),
    )(ids.T, probs.T, tokens, cot)


def masks(pay, count, first, local):
    experts = pay.shape[0] - 2 * count
    named = lax.broadcasted_iota(jnp.int32, (CAP, experts), 1)
    pick = jnp.concatenate([(named == first + i).astype(F32) for i in range(local)], axis=0).astype(BF)
    slot = lax.broadcasted_iota(jnp.int32, (CAP, count), 0).astype(F32)
    slot = jnp.concatenate([slot] * local, axis=0)
    hit = mm(pick, pay[2 * count :, :count]) == slot
    weight = jnp.where(hit, mm(pick, pay[2 * count :, count : 2 * count]), 0.0)
    return hit.astype(F32), weight


def scatter_slots(dst, values, d, local):
    for i in range(local):
        dst[i, d * CAP : (d + 1) * CAP, :] = values[i * CAP : (i + 1) * CAP, :]


def act_gradient(pre, hidden_grad):
    middle = pre.shape[-1] // 2
    g, u = pre[:, :middle], pre[:, middle:]
    s = jax.nn.sigmoid(g)
    return jnp.concatenate(
        [hidden_grad * u * s * (1.0 + g * (1.0 - s)), hidden_grad * g * s], axis=-1
    ).astype(BF)


def stage_kernel(m, own, local, count, after, scal, *refs):
    pays, (wgu, wd) = refs[:m], refs[m : m + 2]
    refs = refs[m + 2 + after :]
    x_ref, h_ref, pg_ref, gs_ref = refs[:4]
    sums, refs = refs[4 : 4 + own], refs[4 + own :]
    xs, hs, gu_s, d_s, sem = refs[:5]
    if own:
        hit_s, wt_s, cs, o_s, dx_s, dots_s = refs[5:]
    e = pl.program_id(0)
    here = pl.ds(pl.multiple_of(e * CAP, CAP), CAP)

    def fetch(k):
        slot = lax.rem(k, 2)
        return (
            pltpu.make_async_copy(wgu.at[k], gu_s.at[slot], sem.at[0, slot]),
            pltpu.make_async_copy(wd.at[k], d_s.at[slot], sem.at[1, slot]),
        )

    @pl.when(e == 0)
    def _():
        for copy in fetch(e):
            copy.start()

    @pl.when(e + 1 < local)
    def _():
        for copy in fetch(e + 1):
            copy.start()

    @pl.when(e == 0)
    def _():
        for d in range(m):
            hit, weight = masks(pays[d], count, scal[0], local)
            hit_b = hit.astype(BF)
            scatter_slots(xs, mm(hit_b, pays[d][:count, :]).astype(BF), d, local)
            if d < own:
                hit_s[d] = hit_b
                wt_s[d] = weight.astype(BF)
                slots = mm(hit_b, pays[d][count : 2 * count, :])
                scatter_slots(cs, slots.astype(BF), d, local)
                slots = jnp.sum(weight, axis=1, keepdims=True) * slots
            else:
                slots = mm(weight.astype(BF), pays[d][count : 2 * count, :])
            scatter_slots(gs_ref, slots.astype(BF), d, local)

    half_d, half_f = x_ref.shape[-1], h_ref.shape[-1]
    x_ref[0] = xs[e, :, pl.ds(pl.multiple_of(scal[1] * half_d, half_d), half_d)]
    for copy in fetch(e):
        copy.wait()
    slot = lax.rem(e, 2)
    pre = mm(xs[e], gu_s[slot])
    middle = pre.shape[-1] // 2
    hidden = (jax.nn.silu(pre[:, :middle]) * pre[:, middle:]).astype(BF)
    hs[...] = hidden
    h_ref[0] = hs[:, pl.ds(pl.multiple_of(scal[1] * half_f, half_f), half_f)]
    pg = act_gradient(pre, mm_t1(gs_ref[e], d_s[slot]))
    pg_ref[0] = pg
    if own:
        out = mm(hidden[: own * CAP], d_s[slot]).astype(BF)
        dots = jnp.sum(cs[e].astype(F32) * out.astype(F32), axis=1, keepdims=True)
        dx = mm_t1(pg[: own * CAP], gu_s[slot]).astype(BF)
        for d in range(own):
            part = slice(d * CAP, (d + 1) * CAP)
            o_s[d, here, :] = out[part]
            dx_s[d, here, :] = dx[part]
            spread = hit_s[d, here, :].astype(F32) * dots[part]
            dots_s[d, pl.ds(e, 1), :] = jnp.sum(spread, axis=0, keepdims=True)

        @pl.when(e == local - 1)
        def _():
            for d in range(own):
                sums[d][:count, :] = mm_t0(wt_s[d], o_s[d]).astype(BF)
                sums[d][count : 2 * count, :] = mm_t0(hit_s[d], dx_s[d]).astype(BF)
                experts, width = sums[d].shape[0] - 2 * count, sums[d].shape[1]
                row = lax.broadcasted_iota(jnp.int32, (experts, count), 0)
                dots = jnp.zeros((experts, count), F32)
                for i in range(local):
                    dots = dots + jnp.where(row == scal[0] + i, dots_s[d, i : i + 1, :], 0.0)
                upper = dots.astype(BF).astype(F32)
                rest = jnp.zeros((experts, width - 2 * count), F32)
                sums[d][2 * count :, :] = jnp.concatenate([upper, dots - upper, rest], axis=1).astype(BF)


def stage(scal, limit, mine, others, count, wgu, wd, after=()):
    pays = (*mine, *others)
    m, own, (local, width, two_f) = len(pays), len(mine), wgu.shape
    rows, ff = m * CAP, two_f // 2
    outs = [
        (jax.ShapeDtypeStruct((local, rows, width // HALVES), BF), per_expert((local, rows, width // HALVES))),
        (jax.ShapeDtypeStruct((local, rows, ff // HALVES), BF), per_expert((local, rows, ff // HALVES))),
        (jax.ShapeDtypeStruct((local, rows, two_f), BF), per_expert((local, rows, two_f))),
        (jax.ShapeDtypeStruct((local, rows, width), BF), full((local, rows, width))),
    ]
    outs += [(jax.ShapeDtypeStruct(a.shape, BF), full(a.shape)) for a in mine]
    scratch = [
        pltpu.VMEM((local, rows, width), BF),
        pltpu.VMEM((rows, ff), BF),
        pltpu.VMEM((2,) + wgu.shape[1:], BF),
        pltpu.VMEM((2,) + wd.shape[1:], BF),
        pltpu.SemaphoreType.DMA((2, 2)),
    ]
    if own:
        scratch += [
            pltpu.VMEM((own, local * CAP, count), BF),
            pltpu.VMEM((own, local * CAP, count), BF),
            pltpu.VMEM((local, own * CAP, width), BF),
            pltpu.VMEM((own, local * CAP, width), BF),
            pltpu.VMEM((own, local * CAP, width), BF),
            pltpu.VMEM((own, local, count), F32),
        ]
    res = pl.pallas_call(
        functools.partial(stage_kernel, m, own, local, count, len(after)),
        grid_spec=pltpu.PrefetchScalarGridSpec(
            num_scalar_prefetch=1,
            grid=(local,),
            in_specs=[full(a.shape) for a in pays]
            + [pl.BlockSpec(memory_space=pl.ANY)] * (2 + len(after)),
            out_specs=[o[1] for o in outs],
            scratch_shapes=scratch,
        ),
        out_shape=[o[0] for o in outs],
        compiler_params=pltpu.CompilerParams(vmem_limit_bytes=limit),
        cost_estimate=pl.CostEstimate(
            flops=(14 if own else 7) * 1000 * 1000 * 1000, bytes_accessed=24 << 20, transcendentals=local * rows * ff
        ),
    )(scal, *pays, wgu, wd, *after)
    return res[:4], list(res[4:])


def send_kernel(parts, low, scal, *refs):
    xs, hs, pgs, gss = (refs[k * parts : (k + 1) * parts] for k in range(4))
    gates, downs, own_down, acc_d = refs[4 * parts : 4 * parts + low - 1], refs[4 * parts + low - 1 : -2], refs[-2], refs[-1]
    lo = scal[2]
    pg = jnp.concatenate([p[0] for p in pgs], axis=0)
    size = xs[0].shape[-1] // low
    for j in range(1, low):
        cols = pl.ds(pl.multiple_of(lax.rem(lo + j, low) * size, size), size)
        gates[j - 1][0] = mm_t0(jnp.concatenate([x[0, :, cols] for x in xs], axis=0), pg).astype(BF)
    h = jnp.concatenate([h_[0] for h_ in hs], axis=0)
    acc_d[...] = mm_t0(h, jnp.concatenate([g[0] for g in gss], axis=0))
    size = acc_d.shape[0] // low
    for j in range(low):
        block = acc_d[pl.ds(pl.multiple_of(lax.rem(lo + j, low) * size, size), size), :]
        if j:
            downs[j - 1][0] = block.astype(BF)
        else:
            own_down[0] = block


def send_blocks(scal, low, stages, start, local, after=()):
    xs, hs, pgs, gss = zip(*stages)
    width, ff = gss[0].shape[-1], pgs[0].shape[-1] // 2
    half_d, half_f = xs[0].shape[-1], hs[0].shape[-1]
    whole = lambda a: pl.BlockSpec((1,) + a.shape[1:], lambda e, s: (e + start, 0, 0))
    gate_shape, down_shape = (local, half_d // low, 2 * ff), (local, half_f // low, width)
    outs = [jax.ShapeDtypeStruct(gate_shape, BF)] * (low - 1)
    outs += [jax.ShapeDtypeStruct(down_shape, BF)] * (low - 1) + [jax.ShapeDtypeStruct(down_shape, F32)]
    k = len(after)
    body = functools.partial(send_kernel, len(stages), low)
    res = pl.pallas_call(
        lambda s, *refs: body(s, *refs[k:]),
        grid_spec=pltpu.PrefetchScalarGridSpec(
            num_scalar_prefetch=1,
            grid=(local,),
            in_specs=[pl.BlockSpec(memory_space=pl.ANY)] * k
            + [whole(a) for a in (*xs, *hs, *pgs, *gss)],
            out_specs=[per_expert(o.shape) for o in outs],
            scratch_shapes=[pltpu.VMEM((half_f, width), F32)],
        ),
        out_shape=outs,
        compiler_params=pltpu.CompilerParams(vmem_limit_bytes=SHARE_VMEM),
        cost_estimate=pl.CostEstimate(
            flops=0, bytes_accessed=1 << 10, transcendentals=0
        ),
    )(scal, *after, *xs, *hs, *pgs, *gss)
    return res[: low - 1], res[low - 1 : 2 * low - 2], res[-1]


def own_kernel(parts, low, scal, *refs):
    xs, pgs, out_ref = refs[:parts], refs[parts : 2 * parts], refs[-1]
    size = xs[0].shape[-1] // low
    cols = pl.ds(pl.multiple_of(scal[2] * size, size), size)
    out_ref[0] = mm_t0(
        jnp.concatenate([x[0, :, cols] for x in xs], axis=0), jnp.concatenate([p[0] for p in pgs], axis=0)
    )


def own_blocks(scal, low, stages, after):
    xs, _, pgs, _ = zip(*stages)
    out = jax.ShapeDtypeStruct((xs[0].shape[0], xs[0].shape[-1] // low, pgs[0].shape[-1]), F32)
    return pl.pallas_call(
        functools.partial(own_kernel, len(stages), low),
        grid_spec=pltpu.PrefetchScalarGridSpec(
            num_scalar_prefetch=1,
            grid=(out.shape[0],),
            in_specs=[per_expert(a.shape) for a in (*xs, *pgs)] + [pl.BlockSpec(memory_space=pl.ANY)] * len(after),
            out_specs=per_expert(out.shape),
        ),
        out_shape=out,
        compiler_params=pltpu.CompilerParams(vmem_limit_bytes=SHARE_VMEM),
        cost_estimate=pl.CostEstimate(flops=0, bytes_accessed=1 << 10, transcendentals=0),
    )(scal, *xs, *pgs, *after)


def join_kernel(pieces, low, own_ref, *refs):
    gate_ref, down_ref = refs[-2:]
    e = 0
    for k in range(pieces):
        arrived = refs[k * (2 * low - 1) : (k + 1) * (2 * low - 1)]
        for i in range(arrived[-1].shape[0]):
            gate_ref[:, e, :] = own_ref[e] + sum(g[i].astype(F32) for g in arrived[: low - 1])
            down_ref[:, e, :] = arrived[-1][i] + sum(g[i].astype(F32) for g in arrived[low - 1 : -1])
            e += 1


def join_blocks(low, own, pieces):
    arrived = [a for piece in pieces for a in piece]
    local, steps = own.shape[0], 4
    lanes = lambda a: pl.BlockSpec(a.shape[:-1] + (a.shape[-1] // steps,), lambda c: (0, 0, c))
    outs = [
        jax.ShapeDtypeStruct((a.shape[1], local, a.shape[-1]), F32) for a in (own, pieces[0][-1])
    ]
    return pl.pallas_call(
        functools.partial(join_kernel, len(pieces), low),
        grid=(steps,),
        in_specs=[lanes(a) for a in (own, *arrived)],
        out_specs=[lanes(o) for o in outs],
        out_shape=outs,
        compiler_params=pltpu.CompilerParams(vmem_limit_bytes=SHARE_VMEM),
        cost_estimate=pl.CostEstimate(flops=5 * 1000 * 1000 * 1000, bytes_accessed=16 << 20, transcendentals=0),
    )(own, *arrived)


def on_device(n, replicas, tokens, expert_ids, gate_probs, cotangent, gate_up, down_weights):
    local, count = gate_up.shape[1], tokens.shape[0]
    low = replicas // HALVES
    z, r = lax.axis_index("expert"), lax.axis_index("replica")
    scal = jnp.stack([z * local, r // low, r % low]).astype(jnp.int32)
    ring = [(i, (i + 1) % n) for i in range(n)]
    across = [(i, (i + low) % replicas) for i in range(replicas)]

    pays = [pack(expert_ids, gate_probs, tokens, cotangent, n * local)]
    others = []
    wgu = jnp.transpose(gate_up, (1, 0, 2))
    for d in range(n):
        others.append(lax.ppermute(pays[d], "replica", across))
        if d < n - 1:
            pays.append(lax.ppermute(pays[d], "expert", ring))
            if d == 0:
                pays[1], others[0], wgu, down_weights = lax.optimization_barrier(
                    (pays[1], others[0], wgu, down_weights)
                )

    wd = jnp.transpose(down_weights, (1, 0, 2))

    def add(got, mine):
        return (got.astype(F32) + mine.astype(F32)).astype(BF)

    step = -(-n // 4)
    stages, sums, totals, before = [], {}, [], ()
    for start in range(0, n, step):
        ready = [d for d in range(start + 1, start + step + 1) if d < n] + ([0] if start == step else [])
        outs, part = stage(scal, EARLY_VMEM if start <= step else STAGE_VMEM, [pays[d] for d in ready], others[start : start + step], count, wgu, wd, before)
        stages.append(outs)
        sums.update(zip(ready, part))
        before = (outs[3],)
        for d in ready:
            if d:
                if totals:
                    send, _ = lax.optimization_barrier((totals[-1], pays[d]))
                    totals.append(add(lax.ppermute(send, "expert", ring), sums[d]))
                else:
                    totals.append(sums[d])
                before = (outs[3], totals[-1])
    steps = [[(i, i // low * low + (i % low + j) % low) for i in range(replicas)] for j in range(1, low)]
    arrived = lax.ppermute(totals[-1], "expert", ring)
    last = local // 2
    pieces, sent = [], ()
    for start, size in ((0, last), (last, local - last)) if last else ((0, local),):
        gates, downs, own_down = send_blocks(scal, low, stages, start, size)
        sent = (*gates, *downs)
        if start:
            gates, downs, arrived = lax.optimization_barrier((gates, downs, arrived))
        gates = [lax.ppermute(b, "replica", s) for b, s in zip(gates, steps)]
        downs = [lax.ppermute(b, "replica", s) for b, s in zip(downs, steps)]
        pieces.append((*gates, *downs, own_down))
    own = own_blocks(scal, low, stages, sent)
    gate_up_gradient, down_gradient = join_blocks(low, own, pieces)
    combined, token_gradient = add(arrived[:count], sums[0][:count]), add(arrived[count : 2 * count], sums[0][count : 2 * count])
    dots = arrived[2 * count :, : 2 * count].astype(F32) + sums[0][2 * count :, : 2 * count].astype(F32)
    dots = dots[:, :count] + dots[:, count:]
    named = expert_ids.T[:, None, :] == jnp.arange(n * local, dtype=jnp.int32)[None, :, None]
    prob_gradient = jnp.sum(jnp.where(named, dots[None], 0.0), axis=1).T
    return (combined, token_gradient, prob_gradient, gate_up_gradient, down_gradient)


def solution(mesh):
    rows = P(("groups", "expert", "replica"), None)
    weights = P(None, "expert", None)
    shares = P(("groups", "replica"), "expert", None)
    return jax.shard_map(
        functools.partial(on_device, mesh.shape["expert"], mesh.shape["replica"]),
        mesh=mesh,
        in_specs=(rows, rows, rows, rows, weights, weights),
        out_specs=(rows, rows, rows, shares, shares),
        check_vma=False,
    )
```
